512 devices in a mesh: dp: 16 (over y, core), expert: 32 (over z, x).
Axes of the slice: x: 4, y: 8, z: 8, core: 2. Of those that a mesh axis runs over, the one named last changes fastest.
Arguments:
- tokens: bfloat16 [65536, 2048], P(('dp', 'expert')), may hold values from -6 to 6
- routes: int32 [65536, 8], P(('dp', 'expert')), may hold values from 0 to 127, as said below
- cotangent: bfloat16 [65536, 8, 384], P(('dp', 'expert')), may hold values from -6 to 6
- gate_weight: bfloat16 [32, 2048, 384], P('expert', 'dp'), may hold values from -0.125 to 0.125
- up_weight: bfloat16 [32, 2048, 384], P('expert', 'dp'), may hold values from -0.125 to 0.125
Outputs:
- token_grad: bfloat16 [65536, 2048], P(('dp', 'expert'))
- gate_grad: float32 [32, 2048, 384], P('expert', 'dp')
- up_grad: float32 [32, 2048, 384], P('expert', 'dp')
The draws below stay inside these ranges and needn't reach their ends.
Inputs may be any that keep to these rules, and one draw needn't show every extreme that they name: `routes`: each row names 8 different experts. In the rows of one device no expert is named by more than 20 rows, and some expert below 32 is named by exactly 20 rows on every device.
All inputs are finite; a program needn't handle non-finite values.
Results may differ from the reference program's by a relative error of at most 0.02.
Values may be sent and summed in bfloat16 or wider, within the bound.
No kernel may reach another device: no remote copies, remote signals or barrier semaphores. Data moves between devices by JAX's collectives and lax.ppermute only.
A program may use at most 64 MiB of HBM per device.

```python
import jax
import jax.numpy as jnp
from jax import lax

D = 2048
EXPERTS = 128
TOP = 8
FW = 384
TOK_DEV = 128
CAP = 20
TOKENS = 65536
N_DP = 16
N_EXPERT = 32


def draw_routes(key, part):
    key = jax.random.fold_in(key, 11)
    perm_key, full_key, label_key, pair_key, shuffle_key, offset_key = jax.random.split(key, 6)
    classes = EXPERTS // TOP
    unit_size = TOK_DEV // 32
    blocks = TOKENS // TOK_DEV
    shuffle = jax.random.permutation(perm_key, EXPERTS).astype(jnp.int32)
    inverse = jnp.zeros((EXPERTS,), jnp.int32).at[shuffle].set(jnp.arange(EXPERTS, dtype=jnp.int32))
    full_expert = jax.random.randint(full_key, (), 0, N_EXPERT)
    anchor = inverse[full_expert] % classes
    labels = jax.vmap(lambda sub_key: jax.random.permutation(sub_key, classes))(jax.random.split(label_key, blocks)).astype(jnp.int32)
    class_rank = (labels - labels[:, anchor][:, None]) % classes
    pair_shift = jax.random.randint(pair_key, (blocks, classes // 2), 0, unit_size + 1)
    shift_value = jnp.take_along_axis(pair_shift, class_rank // 2, axis=1)
    signed_shift = jnp.where(class_rank % 2 == 0, shift_value, -shift_value)
    counts = jnp.where(class_rank < classes // 4, 5 * unit_size, unit_size + signed_shift)
    bounds = jnp.cumsum(counts, axis=1)
    position = jnp.arange(TOK_DEV, dtype=jnp.int32)
    token_class = jnp.sum((position[None, :, None] >= bounds[:, None, :]).astype(jnp.int32), axis=2)
    token_order = jax.vmap(lambda sub_key: jax.random.permutation(sub_key, TOK_DEV))(jax.random.split(shuffle_key, blocks)).astype(jnp.int32)
    token_class = jnp.take_along_axis(token_class, token_order, axis=1)
    offset = jax.random.randint(offset_key, (blocks, TOK_DEV), 0, TOP)
    start_slot = token_class + classes * offset
    slot_table = (start_slot[:, :, None] + classes * jnp.arange(TOP, dtype=jnp.int32)[None, None, :]) % EXPERTS
    expert_ids = shuffle[slot_table]
    return expert_ids.reshape(TOKENS, TOP).astype(jnp.int32)


def levels(key, dims, cuts, low, top_value):
    loudness = 1.0
    for axis_at, blocks in cuts:
        steps = jax.random.uniform(jax.random.fold_in(jax.random.fold_in(key, 6), axis_at), (blocks,), jnp.float32, low / len(cuts), top_value / len(cuts))
        loudness = loudness * jnp.repeat(jnp.exp(steps), dims[axis_at] // blocks).reshape((-1,) + (1,) * (len(dims) - 1 - axis_at))
    return loudness


def scatter_about(rng, dims, scale, bound, cuts=(), kind=jnp.bfloat16):
    level = levels(rng, dims, cuts, -0.22, 0.18) if cuts else 1.0
    entries = jax.random.normal(rng, dims, jnp.float32) * scale * level
    return jnp.minimum(jnp.maximum(entries, -bound), bound).astype(kind)


def setup_inputs(seed: int = 0) -> dict:
    streams_of = jax.random.split(jax.random.key(seed), 6)
    return {
        "tokens": scatter_about(streams_of[0], (TOKENS, D), 1.0, 6.0, ((0, 512),)),
        "routes": draw_routes(jax.random.fold_in(streams_of[5], 71), 0),
        "cotangent": scatter_about(streams_of[2], (TOKENS, TOP, FW), 1.0, 6.0, ((0, 512),)),
        "gate_weight": scatter_about(streams_of[3], (N_EXPERT, D, FW), D ** -0.5, 0.125, ((0, 32), (1, 16))),
        "up_weight": scatter_about(streams_of[4], (N_EXPERT, D, FW), D ** -0.5, 0.125, ((0, 32), (1, 16))),
    }


def reference(tokens, routes, cotangent, gate_weight, up_weight):
    per_group = TOKENS // N_DP
    capacity = N_EXPERT * CAP
    token_groups = tokens.reshape(N_DP, per_group, D)
    route_groups = routes.reshape(N_DP, per_group * TOP)
    cot_groups = cotangent.reshape(N_DP, per_group * TOP, FW)

    def one_expert(token_sum, expert):
        gate_matrix = gate_weight[expert]
        up_matrix = up_weight[expert]

        def one_group(running, group_index):
            token_acc, gate_acc, up_acc = running
            matches = route_groups[group_index] == expert
            positions = jnp.nonzero(matches, size=capacity, fill_value=0)[0].astype(jnp.int32)
            in_window = jnp.arange(capacity, dtype=jnp.int32) < jnp.sum(matches.astype(jnp.int32))
            owner_token = positions // TOP
            token_rows = token_groups[group_index][owner_token]
            grad_out = jnp.where(in_window[:, None], cot_groups[group_index][positions].astype(jnp.float32), 0.0)
            gate_pre = jnp.dot(token_rows, gate_matrix, preferred_element_type=jnp.float32)
            up_pre = jnp.dot(token_rows, up_matrix, preferred_element_type=jnp.float32)
            sigmoid_gate = jax.nn.sigmoid(gate_pre)
            gate_delta = (grad_out * up_pre * sigmoid_gate * (1.0 + gate_pre * (1.0 - sigmoid_gate))).astype(jnp.bfloat16)
            up_delta = (grad_out * gate_pre * sigmoid_gate).astype(jnp.bfloat16)
            slot_grad = (jnp.dot(gate_delta, gate_matrix.T, preferred_element_type=jnp.float32)
                         + jnp.dot(up_delta, up_matrix.T, preferred_element_type=jnp.float32)).astype(jnp.bfloat16)
            slot_grad = lax.optimization_barrier(slot_grad).astype(jnp.float32)
            target = group_index.astype(jnp.int32) * per_group + owner_token
            token_acc = token_acc.at[target].add(slot_grad)
            group_gate = lax.dot_general(token_rows, gate_delta, (((0,), (0,)), ((), ())), preferred_element_type=jnp.float32)
            group_up = lax.dot_general(token_rows, up_delta, (((0,), (0,)), ((), ())), preferred_element_type=jnp.float32)
            group_gate = lax.optimization_barrier(group_gate.astype(jnp.bfloat16)).astype(jnp.float32)
            group_up = lax.optimization_barrier(group_up.astype(jnp.bfloat16)).astype(jnp.float32)
            return (token_acc, gate_acc + group_gate, up_acc + group_up), None

        start = (token_sum, jnp.zeros((D, FW), jnp.float32), jnp.zeros((D, FW), jnp.float32))
        (token_sum, gate_acc, up_acc), unused = lax.scan(one_group, start, jnp.arange(N_DP, dtype=jnp.int32))
        return token_sum, (gate_acc / N_DP, up_acc / N_DP)

    token_sum = jnp.zeros((TOKENS, D), jnp.float32)
    token_sum, (gate_grad, up_grad) = lax.scan(one_expert, token_sum, jnp.arange(N_EXPERT, dtype=jnp.int32))
    return token_sum.astype(jnp.bfloat16), gate_grad, up_grad
```

```python
import jax
import jax.numpy as jnp
from jax import lax
from jax.experimental import pallas as pl
from jax.experimental.pallas import tpu as pltpu
from jax.sharding import PartitionSpec as P

CAP = 20
BLOCK = 24
TAIL = 4
PER_ROW = 5
BACK = 40
VMEM = 40 * 2**20


def iota(shape, axis):
    return lax.broadcasted_iota(jnp.int32, shape, axis)


def one_if(condition):
    return jnp.where(condition, 1.0, 0.0).astype(jnp.bfloat16)


def dot(left, right):
    return jnp.dot(left, right, preferred_element_type=jnp.float32)


def times_transposed(left, right):
    return lax.dot_general(
        left, right, (((1,), (1,)), ((), ())), preferred_element_type=jnp.float32
    )


def ranks(routes, experts):
    top, count = routes.shape
    expert = iota((experts, count), 0)
    routed = jnp.zeros((experts, count), jnp.float32)
    for k in range(top):
        routed += jnp.where(routes[k : k + 1, :] == expert, 1.0, 0.0)
    earlier = one_if(iota((count, count), 0) < iota((count, count), 1))
    rank = dot(routed.astype(jnp.bfloat16), earlier)
    return rank, jnp.where(routed > 0.5, rank, -1.0)


def repeat_rows(experts, rows):
    row = iota((experts * rows, experts), 0)
    first = iota((experts * rows, experts), 1) * rows
    return one_if((row >= first) & (row < first + rows))


def pack_kernel(experts, routes_ref, tokens_ref, cot_ref, out_ref):
    routes = routes_ref[...]
    top, count = routes.shape
    width = tokens_ref.shape[1]
    hidden = cot_ref.shape[1]
    rank, place = ranks(routes, experts)
    at = dot(repeat_rows(experts, BLOCK), place.astype(jnp.bfloat16))
    row = iota((experts, BLOCK, count), 1).reshape(experts * BLOCK, count)
    pick = one_if(at == row.astype(jnp.float32))
    slots = count * top
    spread = one_if(lax.shift_right_logical(iota((count, slots), 1), 3) == iota((count, slots), 0))
    both = jnp.concatenate((routes.astype(jnp.float32), rank), axis=0).astype(jnp.bfloat16)
    wide = dot(both, spread)
    own = iota((top, slots), 0) == (iota((top, slots), 1) & (top - 1))
    named = jnp.sum(jnp.where(own, wide[:top], 0.0), axis=0, keepdims=True)
    slot_place = jnp.where(
        named == iota((experts, slots), 0).astype(jnp.float32), wide[top:], -1.0
    )
    slot_at = dot(repeat_rows(experts, 8), slot_place.astype(jnp.bfloat16))
    tail_row = iota((experts, 8, slots), 1).reshape(experts * 8, slots) - TAIL
    offset = jnp.where(tail_row >= 0, slot_at - tail_row.astype(jnp.float32), -1.0)
    cot = cot_ref[...]
    for i in range(PER_ROW + 1):
        low, high = i * hidden, min((i + 1) * hidden, width)
        rows = dot(pick, tokens_ref[:, low:high])
        if i < PER_ROW:
            tail = dot(one_if(offset == float(TAIL * i)), cot)
            rows = rows.reshape(experts, BLOCK, hidden)
            last = rows[:, BLOCK - 8 :] + tail.reshape(experts, 8, hidden)
            rows = jnp.concatenate((rows[:, : BLOCK - 8], last), axis=1)
            rows = rows.reshape(experts * BLOCK, hidden)
        out_ref[:, low:high] = rows.astype(jnp.bfloat16)


def combine_matrix_kernel(experts, routes_ref, out_ref):
    _, place = ranks(routes_ref[...], experts)
    count = place.shape[1]
    lane = iota((experts, experts * BACK), 1)
    first = iota((experts, experts * BACK), 0) * BACK
    mine = (lane >= first) & (lane < first + BACK)
    at = dot(place.T.astype(jnp.bfloat16), one_if(mine))
    within = jnp.sum(jnp.where(mine, lane - first, 0), axis=0, keepdims=True).astype(jnp.float32)
    low = jnp.where(within < CAP, within, -2.0)
    high = jnp.where(within < BLOCK, within - TAIL, within - BLOCK)
    high = jnp.where(within < CAP, -2.0, high)
    out_ref[:count] = one_if(at == low)
    out_ref[count:] = one_if(at == high)


def middle_kernel(received_ref, weight_ref, delta_ref, back_ref):
    rows, width = received_ref.shape
    hidden = weight_ref.shape[1] // 2
    blocks = rows // BLOCK
    received = received_ref[...]
    pre = dot(received, weight_ref[...])
    gate_pre, up_pre = pre[:, :hidden], pre[:, hidden:]
    tail = received.astype(jnp.float32).reshape(blocks, BLOCK, width)[:, BLOCK - 8 :]
    first = iota((blocks, 8, hidden), 1) < TAIL

    def cot(i):
        return tail[:, :, i * hidden : (i + 1) * hidden]

    grad_out = jnp.concatenate(
        (
            jnp.where(first, pltpu.roll(cot(0), TAIL, 1), cot(1)),
            jnp.where(first, pltpu.roll(cot(2), TAIL, 1), cot(3)),
            jnp.where(first, pltpu.roll(cot(4), TAIL, 1), 0.0),
        ),
        axis=1,
    ).reshape(rows, hidden)
    sigmoid_gate = jax.nn.sigmoid(gate_pre)
    gate_delta = grad_out * up_pre * sigmoid_gate * (1.0 + gate_pre * (1.0 - sigmoid_gate))
    up_delta = grad_out * gate_pre * sigmoid_gate
    delta = jnp.concatenate((gate_delta, up_delta), axis=1)
    delta_ref[...] = delta.astype(jnp.bfloat16)
    delta = delta.reshape(blocks, BLOCK, 2 * hidden)
    last = delta[:, BLOCK - 8 :]
    first = iota(last.shape, 1) < TAIL
    last = jnp.where(first, last, pltpu.roll(last, TAIL, 1))
    delta = jnp.concatenate((delta[:, : BLOCK - 8], last), axis=1)
    delta = delta.reshape(rows, 2 * hidden).astype(jnp.bfloat16)
    half = width // 2
    low = times_transposed(delta, weight_ref[:half]).reshape(blocks, BLOCK, half)
    high = times_transposed(delta, weight_ref[half:]).reshape(blocks, BLOCK, half)
    full = BLOCK - 8
    shared = jnp.where(iota((blocks, 8, half), 1) < TAIL, low[:, full:], high[:, full:])
    back = jnp.concatenate((low[:, :full], shared, high[:, :full]), axis=1)
    back_ref[...] = back.reshape(blocks * BACK, half).astype(jnp.bfloat16)


def combine_kernel(matrix_ref, returned_ref, out_ref):
    count = out_ref.shape[0]
    half = returned_ref.shape[1]
    returned = returned_ref[...]
    out_ref[:, :half] = dot(matrix_ref[:count], returned).astype(jnp.bfloat16)
    out_ref[:, half:] = dot(matrix_ref[count:], returned).astype(jnp.bfloat16)


def whole():
    return pl.BlockSpec(memory_space=pltpu.VMEM)


def call(kernel, out_shape, flops, moved, vmem=VMEM, **more):
    return pl.pallas_call(
        kernel,
        out_shape=out_shape,
        compiler_params=pltpu.CompilerParams(vmem_limit_bytes=vmem),
        cost_estimate=pl.CostEstimate(flops=flops, bytes_accessed=moved, transcendentals=0),
        **more,
    )


def on_device(tokens, routes, cotangent, gate_weight, up_weight):
    peers = lax.axis_size("expert")
    groups = lax.axis_size("dp")
    count, width = tokens.shape
    top = routes.shape[1]
    hidden = cotangent.shape[2]
    half = width // 2
    share = width // groups
    bf16 = jnp.bfloat16
    routes = routes.T
    stacked = jnp.concatenate((gate_weight[0], up_weight[0]), axis=1)
    weight = lax.all_gather(stacked, "dp", axis=0, tiled=True)
    rows = peers * BLOCK
    packed = call(
        lambda *refs: pack_kernel(peers, *refs),
        jax.ShapeDtypeStruct((rows, width), bf16),
        3 * 10**9,
        5 * 10**6,
        60 * 2**20,
        in_specs=[whole()] * 3,
        out_specs=whole(),
    )(routes, tokens, cotangent.reshape(count * top, hidden))
    received = lax.all_to_all(
        packed.reshape(peers, BLOCK, width), "expert", split_axis=0, concat_axis=0, tiled=True
    ).reshape(rows, width)
    matrix = call(
        lambda *refs: combine_matrix_kernel(peers, *refs),
        jax.ShapeDtypeStruct((2 * count, peers * BACK), bf16),
        10**8,
        10**6,
        in_specs=[whole()],
        out_specs=whole(),
    )(routes)
    steps = 2
    delta, back = call(
        middle_kernel,
        (
            jax.ShapeDtypeStruct((rows, 2 * hidden), bf16),
            jax.ShapeDtypeStruct((peers * BACK, half), bf16),
        ),
        5 * 10**9,
        10**7,
        grid=(steps,),
        in_specs=[
            pl.BlockSpec((rows // steps, width), lambda i: (i, 0)),
            pl.BlockSpec((width, 2 * hidden), lambda i: (0, 0)),
        ],
        out_specs=(
            pl.BlockSpec((rows // steps, 2 * hidden), lambda i: (i, 0)),
            pl.BlockSpec((peers * BACK // steps, half), lambda i: (i, 0)),
        ),
    )(received, weight)
    returned = lax.all_to_all(
        back.reshape(peers, BACK, half), "expert", split_axis=0, concat_axis=0, tiled=True
    ).reshape(peers * BACK, half)
    token_grad = call(
        combine_kernel,
        jax.ShapeDtypeStruct((count, width), bf16),
        10**9,
        4 * 10**6,
        in_specs=[whole()] * 2,
        out_specs=whole(),
    )(matrix, returned)
    weight_grad = lax.dot_general(
        received, delta, (((0,), (0,)), ((), ())), preferred_element_type=jnp.float32
    ).astype(bf16)
    summed = lax.psum_scatter(weight_grad, "dp", scatter_dimension=0, tiled=True)
    summed = summed.astype(jnp.float32) * (1.0 / groups)
    gate_grad = summed[:, :hidden].reshape(1, share, hidden)
    up_grad = summed[:, hidden:].reshape(1, share, hidden)
    return (token_grad, gate_grad, up_grad)


def solution(mesh):
    placed = (
        P(("dp", "expert"), None),
        P(("dp", "expert"), None),
        P(("dp", "expert"), None, None),
        P("expert", "dp", None),
        P("expert", "dp", None),
    )
    return jax.shard_map(
        on_device,
        mesh=mesh,
        in_specs=placed,
        out_specs=(P(("dp", "expert"), None), P("expert", "dp", None), P("expert", "dp", None)),
        check_vma=False,
    )
```

```python
import jax
import jax.numpy as jnp
from jax import lax
from jax.experimental import pallas as pl
from jax.experimental.pallas import tpu as pltpu
from jax.sharding import PartitionSpec as P

CAP = 20
BLOCK = 24
TAIL = 4
PER_ROW = 5
BACK = 40
STEPS = 2
CORES = 2
FETCHES = 4
VMEM = 32 * 2**20
BIG = 60 * 2**20
MIDDLE = 46 * 2**20


def iota(shape, axis):
    return lax.broadcasted_iota(jnp.int32, shape, axis)


def one_if(condition):
    return jnp.where(condition, 1.0, 0.0).astype(jnp.bfloat16)


def dot(left, right):
    return jnp.dot(left, right, preferred_element_type=jnp.float32)


def times_transposed(left, right):
    return lax.dot_general(
        left, right, (((1,), (1,)), ((), ())), preferred_element_type=jnp.float32
    )


def transposed_times(left, right):
    return lax.dot_general(
        left, right, (((0,), (0,)), ((), ())), preferred_element_type=jnp.float32
    )


def ranks(routes, experts):
    top, count = routes.shape
    expert = iota((experts, count), 0)
    routed = jnp.zeros((experts, count), jnp.float32)
    for k in range(top):
        routed += jnp.where(routes[k : k + 1, :] == expert, 1.0, 0.0)
    earlier = one_if(iota((count, count), 0) < iota((count, count), 1))
    rank = dot(routed.astype(jnp.bfloat16), earlier)
    return rank, jnp.where(routed > 0.5, rank, -1.0)


def repeat_rows(experts, rows):
    row = iota((experts * rows, experts), 0)
    first = iota((experts * rows, experts), 1) * rows
    return one_if((row >= first) & (row < first + rows))


def pack_kernel(experts, routes_ref, tokens_ref, cot_ref, out_ref, held, sems):
    routes = routes_ref[...]
    top, count = routes.shape
    width = tokens_ref.shape[1]
    hidden = cot_ref.shape[1]
    rank, place = ranks(routes, experts)
    at = dot(repeat_rows(experts, BLOCK), place.astype(jnp.bfloat16))
    row = iota((experts, BLOCK, count), 1).reshape(experts * BLOCK, count)
    pick = one_if(at == row.astype(jnp.float32))
    slots = count * top
    spread = one_if(lax.shift_right_logical(iota((count, slots), 1), 3) == iota((count, slots), 0))
    both = jnp.concatenate((routes.astype(jnp.float32), rank), axis=0).astype(jnp.bfloat16)
    wide = dot(both, spread)
    own = iota((top, slots), 0) == (iota((top, slots), 1) & (top - 1))
    named = jnp.sum(jnp.where(own, wide[:top], 0.0), axis=0, keepdims=True)
    slot_place = jnp.where(
        named == iota((experts, slots), 0).astype(jnp.float32), wide[top:], -8.0
    )
    slot_at = dot(repeat_rows(experts, TAIL), slot_place.astype(jnp.bfloat16))
    offset = slot_at - (iota(slot_at.shape, 0) & (TAIL - 1)).astype(jnp.float32)
    cot = cot_ref[...]
    copies = []
    for i in range(PER_ROW + 1):
        low, high = i * hidden, min((i + 1) * hidden, width)
        rows = dot(pick, tokens_ref[:, low:high])
        if i < PER_ROW:
            tail = dot(one_if(offset == float(TAIL * i)), cot).reshape(experts // 2, 8, hidden)
            tail = jnp.stack((pltpu.roll(tail, TAIL, 1), tail), axis=1).reshape(experts, 8, hidden)
            rows = rows.reshape(experts, BLOCK, hidden)
            last = rows[:, BLOCK - 8 :]
            last = jnp.where(iota(last.shape, 1) < TAIL, last, tail)
            rows = jnp.concatenate((rows[:, : BLOCK - 8], last), axis=1)
            rows = rows.reshape(experts * BLOCK, hidden)
        held[:, low:high] = rows.astype(jnp.bfloat16)
        at = pl.ds(low, high - low)
        copy = pltpu.make_async_copy(held.at[:, at], out_ref.at[:, at], sems.at[i])
        copy.start()
        copies.append(copy)
    for copy in copies:
        copy.wait()


def prepare_kernel(experts, routes_ref, gate_ref, up_ref, out_ref, stacked_ref):
    _, place = ranks(routes_ref[...], experts)
    count = place.shape[1]
    lane = iota((experts, experts * BACK), 1)
    first = iota((experts, experts * BACK), 0) * BACK
    mine = (lane >= first) & (lane < first + BACK)
    at = dot(place.T.astype(jnp.bfloat16), one_if(mine))
    within = jnp.sum(jnp.where(mine, lane - first, 0), axis=0, keepdims=True).astype(jnp.float32)
    low = jnp.where(within < CAP, within, -2.0)
    high = jnp.where(within < BLOCK, within - TAIL, within - BLOCK)
    high = jnp.where(within < CAP, -2.0, high)
    out_ref[:count] = one_if(at == low)
    out_ref[count:] = one_if(at == high)
    stacked_ref[...] = jnp.concatenate((gate_ref[...], up_ref[...]), axis=1)


def middle_kernel(received_ref, source_ref, delta_ref, back_ref, held, sems, weight_ref, weight_sems):
    rows = received_ref.shape[0] // STEPS
    width = received_ref.shape[1]
    hidden = weight_ref.shape[1] // 2
    blocks = rows // BLOCK
    half = width // 2
    full = BLOCK - 8
    copies = []
    depth = width // FETCHES
    fetches = []
    for k in range(FETCHES):
        at = pl.ds(k * depth, depth)
        fetch = pltpu.make_async_copy(source_ref.at[at], weight_ref.at[at], weight_sems.at[k])
        fetch.start()
        fetches.append(fetch)
    for step in range(STEPS):
        part = slice(step * rows, (step + 1) * rows)
        received = received_ref[part]
        pre = jnp.zeros((rows, 2 * hidden), jnp.float32)
        for k, fetch in enumerate(fetches):
            if step == 0:
                fetch.wait()
            at = slice(k * depth, (k + 1) * depth)
            pre += dot(received[:, at], weight_ref[at])
        gate_pre, up_pre = pre[:, :hidden], pre[:, hidden:]
        tail = received.astype(jnp.float32).reshape(blocks, BLOCK, width)[:, full:]
        first = iota((blocks, 8, hidden), 1) < TAIL

        def cot(i, tail=tail):
            return tail[:, :, i * hidden : (i + 1) * hidden]

        grad_out = jnp.concatenate(
            (
                jnp.where(first, pltpu.roll(cot(0), TAIL, 1), cot(1)),
                jnp.where(first, pltpu.roll(cot(2), TAIL, 1), cot(3)),
                jnp.where(first, pltpu.roll(cot(4), TAIL, 1), 0.0),
            ),
            axis=1,
        ).reshape(rows, hidden)
        sigmoid_gate = jax.nn.sigmoid(gate_pre)
        gate_delta = grad_out * up_pre * sigmoid_gate * (1.0 + gate_pre * (1.0 - sigmoid_gate))
        up_delta = grad_out * gate_pre * sigmoid_gate
        delta = jnp.concatenate((gate_delta, up_delta), axis=1)
        delta_ref[part] = delta.astype(jnp.bfloat16)
        delta = delta.reshape(blocks, BLOCK, 2 * hidden)
        last = delta[:, full:]
        last = jnp.where(iota(last.shape, 1) < TAIL, last, pltpu.roll(last, TAIL, 1))
        delta = jnp.concatenate((delta[:, :full], last), axis=1)
        delta = delta.reshape(rows, 2 * hidden).astype(jnp.bfloat16)
        low = times_transposed(delta, weight_ref[:half]).reshape(blocks, BLOCK, half)
        high = times_transposed(delta, weight_ref[half:]).reshape(blocks, BLOCK, half)
        shared = jnp.where(iota((blocks, 8, half), 1) < TAIL, low[:, full:], high[:, full:])
        back = jnp.concatenate((low[:, :full], shared, high[:, :full]), axis=1)
        size = blocks * BACK
        held[step * size : (step + 1) * size] = back.reshape(size, half).astype(jnp.bfloat16)
        at = pl.ds(step * size, size)
        copy = pltpu.make_async_copy(held.at[at], back_ref.at[at], sems.at[step])
        copy.start()
        copies.append(copy)
    for copy in copies:
        copy.wait()


def combine_kernel(matrix_ref, returned_ref, out_ref):
    count = out_ref.shape[0]
    half = returned_ref.shape[1]
    returned = returned_ref[...]
    out_ref[:, :half] = dot(matrix_ref[:count], returned).astype(jnp.bfloat16)
    out_ref[:, half:] = dot(matrix_ref[count:], returned).astype(jnp.bfloat16)


def aligned(index, size):
    return pl.ds(pl.multiple_of(index * size, size), size)


def collect_kernel(place_ref, *refs):
    *blocks, out_ref = refs
    size = blocks[0].shape[0]
    for k, block in enumerate(blocks):
        at = lax.rem(place_ref[0] + len(blocks) - k, len(blocks))
        out_ref[aligned(at, size)] = block[...]


def assemble_kernel(size, place_ref, mine_ref, other_ref, out_ref):
    core = place_ref[1]
    for y in range(mine_ref.shape[0] // size):
        rows = slice(y * size, (y + 1) * size)
        out_ref[aligned(CORES * y + core, size)] = mine_ref[rows]
        out_ref[aligned(CORES * y + 1 - core, size)] = other_ref[rows]


def weight_grad_kernel(other, share, place_ref, received_ref, delta_ref, out_ref):
    core = 1 - place_ref[1] if other else place_ref[1]
    delta = delta_ref[...]
    batch = min(4, out_ref.shape[0] // share)
    for first in range(0, out_ref.shape[0] // share, batch):
        columns = [
            received_ref[:, aligned(CORES * y + core, share)] for y in range(first, first + batch)
        ]
        grad = transposed_times(jnp.concatenate(columns, axis=1), delta)
        out_ref[first * share : (first + batch) * share] = grad.astype(jnp.bfloat16)


def add_kernel(place_ref, mine_ref, other_ref, *out_refs):
    size = out_refs[0].shape[0]
    for k, out_ref in enumerate(out_refs):
        at = aligned(lax.rem(place_ref[0] + k, len(out_refs)), size)
        total = mine_ref[at].astype(jnp.float32) + other_ref[at].astype(jnp.float32)
        out_ref[...] = total.astype(jnp.bfloat16)


def total_kernel(groups, *refs):
    *terms, gate_ref, up_ref = refs
    hidden = gate_ref.shape[1]
    total = terms[0][...].astype(jnp.float32)
    for term in terms[1:]:
        total += term[...].astype(jnp.float32)
    total *= 1.0 / groups
    gate_ref[...] = total[:, :hidden]
    up_ref[...] = total[:, hidden:]


def whole():
    return pl.BlockSpec(memory_space=pltpu.VMEM)


def in_hbm():
    return pl.BlockSpec(memory_space=pltpu.HBM)


def call(kernel, out_shape, flops, moved, vmem=VMEM, **more):
    return pl.pallas_call(
        kernel,
        out_shape=out_shape,
        compiler_params=pltpu.CompilerParams(vmem_limit_bytes=vmem),
        cost_estimate=pl.CostEstimate(flops=flops, bytes_accessed=moved, transcendentals=0),
        **more,
    )


def held_and_sems(shape, count):
    return [pltpu.VMEM(shape, jnp.bfloat16), pltpu.SemaphoreType.DMA((count,))]


def on_device(tokens, routes, cotangent, gate_weight, up_weight):
    peers = lax.axis_size("expert")
    groups = lax.axis_size("dp")
    ys = groups // CORES
    count, width = tokens.shape
    top = routes.shape[1]
    hidden = cotangent.shape[2]
    share = width // groups
    half = width // 2
    bf16 = jnp.bfloat16
    rows = peers * BLOCK
    routes = routes.T
    mine = lax.axis_index("dp")
    place = jnp.stack((mine // CORES, mine % CORES)).astype(jnp.int32)
    scalars = pl.BlockSpec(memory_space=pltpu.SMEM)

    def shape(*dims, kind=bf16):
        return jax.ShapeDtypeStruct(dims, kind)

    def exchange(block, size):
        out = lax.all_to_all(
            block.reshape(peers, size, -1), "expert", split_axis=0, concat_axis=0, tiled=True
        )
        return out.reshape(peers * size, -1)

    def along_y(block, k):
        pairs = [
            (y * CORES + c, (y + k) % ys * CORES + c) for y in range(ys) for c in range(CORES)
        ]
        return lax.ppermute(block, "dp", pairs)

    def other_core(block):
        return lax.ppermute(block, "dp", [(d, d ^ 1) for d in range(groups)])

    packed = call(
        lambda *refs: pack_kernel(peers, *refs),
        shape(rows, width),
        2 * 10**9,
        5 * 10**6,
        BIG,
        in_specs=[whole()] * 3,
        out_specs=in_hbm(),
        scratch_shapes=held_and_sems((rows, width), PER_ROW + 1),
    )(routes, tokens, cotangent.reshape(count * top, hidden))
    received = exchange(packed, BLOCK)
    matrix, stacked = call(
        lambda *refs: prepare_kernel(peers, *refs),
        (shape(2 * count, peers * BACK), shape(share, 2 * hidden)),
        2 * 10**9,
        10**6,
        in_specs=[whole()] * 3,
        out_specs=(whole(), whole()),
    )(routes, gate_weight[0], up_weight[0])
    blocks = [stacked] + [along_y(stacked, k) for k in range(1, ys)]
    of_core = call(
        collect_kernel,
        shape(ys * share, 2 * hidden),
        10**6,
        3 * 10**6,
        in_specs=[scalars] + [whole()] * ys,
        out_specs=whole(),
    )(place, *blocks)
    weight = call(
        lambda *refs: assemble_kernel(share, *refs),
        shape(width, 2 * hidden),
        10**6,
        6 * 10**6,
        in_specs=[scalars] + [whole()] * 2,
        out_specs=whole(),
    )(place, of_core, other_core(of_core))
    delta, back = call(
        middle_kernel,
        (shape(rows, 2 * hidden), shape(peers * BACK, half)),
        5 * 10**9,
        10**7,
        MIDDLE,
        in_specs=[whole(), pl.BlockSpec(memory_space=pl.ANY)],
        out_specs=(whole(), in_hbm()),
        scratch_shapes=held_and_sems((peers * BACK, half), STEPS)
        + held_and_sems((width, 2 * hidden), FETCHES),
    )(received, weight)
    returned = exchange(back, BACK)
    grads = [
        call(
            lambda *refs, other=other: weight_grad_kernel(other, share, *refs),
            shape(ys * share, 2 * hidden),
            2 * 10**9,
            5 * 10**6,
            in_specs=[scalars] + [whole()] * 2,
            out_specs=whole(),
        )(place, received, delta)
        for other in (True, False)
    ]
    sums = call(
        add_kernel,
        (shape(share, 2 * hidden),) * ys,
        10**6,
        5 * 10**6,
        in_specs=[scalars] + [whole()] * 2,
        out_specs=(whole(),) * ys,
    )(place, grads[1], other_core(grads[0]))
    terms = [sums[0]] + [along_y(sums[k], k) for k in range(1, ys)]
    weight_shape = shape(share, hidden, kind=jnp.float32)
    gate_grad, up_grad = call(
        lambda *refs: total_kernel(groups, *refs),
        (weight_shape, weight_shape),
        10**6,
        2 * 10**6,
        in_specs=[whole()] * ys,
        out_specs=(whole(), whole()),
    )(*terms)
    token_grad = call(
        combine_kernel,
        shape(count, width),
        10**9,
        4 * 10**6,
        in_specs=[whole()] * 2,
        out_specs=whole(),
    )(matrix, returned)
    return (token_grad, gate_grad[None], up_grad[None])


def solution(mesh):
    placed = (
        P(("dp", "expert"), None),
        P(("dp", "expert"), None),
        P(("dp", "expert"), None, None),
        P("expert", "dp", None),
        P("expert", "dp", None),
    )
    return jax.shard_map(
        on_device,
        mesh=mesh,
        in_specs=placed,
        out_specs=(P(("dp", "expert"), None), P("expert", "dp", None), P("expert", "dp", None)),
        check_vma=False,
    )
```

```python
import jax
import jax.numpy as jnp
from jax import lax
from jax.experimental import pallas as pl
from jax.experimental.pallas import tpu as pltpu
from jax.sharding import PartitionSpec as P

CAP = 20
BLOCK = 24
TAIL = 4
PER_ROW = 5
BACK = 40
STEPS = 2
CORES = 2
FETCHES = 4
VMEM = 32 * 2**20
BIG = 60 * 2**20
MIDDLE = 32 * 2**20


def iota(shape, axis):
    return lax.broadcasted_iota(jnp.int32, shape, axis)


def one_if(condition):
    return jnp.where(condition, 1.0, 0.0).astype(jnp.bfloat16)


def dot(left, right):
    return jnp.dot(left, right, preferred_element_type=jnp.float32)


def times_transposed(left, right):
    return lax.dot_general(
        left, right, (((1,), (1,)), ((), ())), preferred_element_type=jnp.float32
    )


def transposed_times(left, right):
    return lax.dot_general(
        left, right, (((0,), (0,)), ((), ())), preferred_element_type=jnp.float32
    )


def ranks(routes, experts):
    top, count = routes.shape
    expert = iota((experts, count), 0)
    routed = jnp.zeros((experts, count), jnp.float32)
    for k in range(top):
        routed += jnp.where(routes[k : k + 1, :] == expert, 1.0, 0.0)
    earlier = one_if(iota((count, count), 0) < iota((count, count), 1))
    rank = dot(routed.astype(jnp.bfloat16), earlier)
    return rank, jnp.where(routed > 0.5, rank, -1.0)


def repeat_rows(experts, rows):
    row = iota((experts * rows, experts), 0)
    first = iota((experts * rows, experts), 1) * rows
    return one_if((row >= first) & (row < first + rows))


def pack_kernel(experts, routes_ref, tokens_hbm, cot_hbm, out_ref, held, sems, tokens_ref, cot_ref, in_sems):
    fetches = (
        pltpu.make_async_copy(tokens_hbm, tokens_ref, in_sems.at[0]),
        pltpu.make_async_copy(cot_hbm, cot_ref, in_sems.at[1]),
    )
    for fetch in fetches:
        fetch.start()
    routes = routes_ref[...]
    top, count = routes.shape
    width = tokens_ref.shape[1]
    hidden = cot_ref.shape[1]
    rank, place = ranks(routes, experts)
    at = dot(repeat_rows(experts, BLOCK), place.astype(jnp.bfloat16))
    row = iota((experts, BLOCK, count), 1).reshape(experts * BLOCK, count)
    pick = one_if(at == row.astype(jnp.float32))
    slots = count * top
    spread = one_if(lax.shift_right_logical(iota((count, slots), 1), 3) == iota((count, slots), 0))
    both = jnp.concatenate((routes.astype(jnp.float32), rank), axis=0).astype(jnp.bfloat16)
    wide = dot(both, spread)
    own = iota((top, slots), 0) == (iota((top, slots), 1) & (top - 1))
    named = jnp.sum(jnp.where(own, wide[:top], 0.0), axis=0, keepdims=True)
    slot_place = jnp.where(
        named == iota((experts, slots), 0).astype(jnp.float32), wide[top:], -8.0
    )
    slot_at = dot(repeat_rows(experts, TAIL), slot_place.astype(jnp.bfloat16))
    offset = slot_at - (iota(slot_at.shape, 0) & (TAIL - 1)).astype(jnp.float32)
    for fetch in fetches:
        fetch.wait()
    cot = cot_ref[...]
    copies = []
    for i in range(PER_ROW + 1):
        low, high = i * hidden, min((i + 1) * hidden, width)
        rows = dot(pick, tokens_ref[:, low:high])
        if i < PER_ROW:
            tail = dot(one_if(offset == float(TAIL * i)), cot).reshape(experts // 2, 8, hidden)
            tail = jnp.stack((pltpu.roll(tail, TAIL, 1), tail), axis=1).reshape(experts, 8, hidden)
            rows = rows.reshape(experts, BLOCK, hidden)
            last = rows[:, BLOCK - 8 :]
            last = jnp.where(iota(last.shape, 1) < TAIL, last, tail)
            rows = jnp.concatenate((rows[:, : BLOCK - 8], last), axis=1)
            rows = rows.reshape(experts * BLOCK, hidden)
        held[:, low:high] = rows.astype(jnp.bfloat16)
        at = pl.ds(low, high - low)
        copy = pltpu.make_async_copy(held.at[:, at], out_ref.at[:, at], sems.at[i])
        copy.start()
        copies.append(copy)
    for copy in copies:
        copy.wait()


def stack_kernel(gate_ref, up_ref, stacked_ref):
    stacked_ref[...] = jnp.concatenate((gate_ref[...], up_ref[...]), axis=1)


def combine_kernel(experts, routes_ref, returned_ref, out_ref):
    _, place = ranks(routes_ref[...], experts)
    half = returned_ref.shape[1]
    lane = iota((experts, experts * BACK), 1)
    first = iota((experts, experts * BACK), 0) * BACK
    mine = (lane >= first) & (lane < first + BACK)
    at = dot(place.T.astype(jnp.bfloat16), one_if(mine))
    within = jnp.sum(jnp.where(mine, lane - first, 0), axis=0, keepdims=True).astype(jnp.float32)
    low = jnp.where(within < CAP, within, -2.0)
    high = jnp.where(within < BLOCK, within - TAIL, within - BLOCK)
    high = jnp.where(within < CAP, -2.0, high)
    returned = returned_ref[...]
    out_ref[:, :half] = dot(one_if(at == low), returned).astype(jnp.bfloat16)
    out_ref[:, half:] = dot(one_if(at == high), returned).astype(jnp.bfloat16)


def middle_kernel(
    received_ref, weight_hbm, delta_hbm, back_hbm, weight_ref, in_sems, delta_ref, delta_sems, held, sems, pre_ref
):
    rows = received_ref.shape[0] // STEPS
    width = received_ref.shape[1]
    hidden = weight_ref.shape[1] // 2
    blocks = rows // BLOCK
    half = width // 2
    full = BLOCK - 8
    depth = width // FETCHES
    fetches, copies = [], []
    for k in range(FETCHES):
        at = pl.ds(k * depth, depth)
        fetch = pltpu.make_async_copy(weight_hbm.at[at], weight_ref.at[at], in_sems.at[k])
        fetch.start()
        fetches.append(fetch)
    for k, fetch in enumerate(fetches):
        fetch.wait()
        at = slice(k * depth, (k + 1) * depth)
        pre = dot(received_ref[:, at], weight_ref[at])
        pre_ref[...] = pre if k == 0 else pre_ref[...] + pre
    for step in range(STEPS):
        part = slice(step * rows, (step + 1) * rows)
        received = received_ref[part]
        pre = pre_ref[part]
        gate_pre, up_pre = pre[:, :hidden], pre[:, hidden:]
        tail = received.astype(jnp.float32).reshape(blocks, BLOCK, width)[:, full:]
        first = iota((blocks, 8, hidden), 1) < TAIL

        def cot(i, tail=tail):
            return tail[:, :, i * hidden : (i + 1) * hidden]

        grad_out = jnp.concatenate(
            (
                jnp.where(first, pltpu.roll(cot(0), TAIL, 1), cot(1)),
                jnp.where(first, pltpu.roll(cot(2), TAIL, 1), cot(3)),
                jnp.where(first, pltpu.roll(cot(4), TAIL, 1), 0.0),
            ),
            axis=1,
        ).reshape(rows, hidden)
        sigmoid_gate = jax.nn.sigmoid(gate_pre)
        gate_delta = grad_out * up_pre * sigmoid_gate * (1.0 + gate_pre * (1.0 - sigmoid_gate))
        up_delta = grad_out * gate_pre * sigmoid_gate
        delta = jnp.concatenate((gate_delta, up_delta), axis=1)
        delta_ref[part] = delta.astype(jnp.bfloat16)
        at = pl.ds(step * rows, rows)
        copy = pltpu.make_async_copy(delta_ref.at[at], delta_hbm.at[at], delta_sems.at[step])
        copy.start()
        copies.append(copy)
        delta = delta.reshape(blocks, BLOCK, 2 * hidden)
        last = delta[:, full:]
        last = jnp.where(iota(last.shape, 1) < TAIL, last, pltpu.roll(last, TAIL, 1))
        delta = jnp.concatenate((delta[:, :full], last), axis=1)
        delta = delta.reshape(rows, 2 * hidden).astype(jnp.bfloat16)
        low = times_transposed(delta, weight_ref[:half]).reshape(blocks, BLOCK, half)
        high = times_transposed(delta, weight_ref[half:]).reshape(blocks, BLOCK, half)
        shared = jnp.where(iota((blocks, 8, half), 1) < TAIL, low[:, full:], high[:, full:])
        back = jnp.concatenate((low[:, :full], shared, high[:, :full]), axis=1)
        size = blocks * BACK
        held[step * size : (step + 1) * size] = back.reshape(size, half).astype(jnp.bfloat16)
        at = pl.ds(step * size, size)
        copy = pltpu.make_async_copy(held.at[at], back_hbm.at[at], sems.at[step])
        copy.start()
        copies.append(copy)
    for copy in copies:
        copy.wait()


def aligned(index, size):
    return pl.ds(pl.multiple_of(index * size, size), size)


def collect_kernel(place_ref, *refs):
    *blocks, out_ref = refs
    size = blocks[0].shape[0]
    for k, block in enumerate(blocks):
        at = lax.rem(place_ref[0] + len(blocks) - k, len(blocks))
        out_ref[aligned(at, size)] = block[...]


def assemble_kernel(size, place_ref, mine_ref, other_ref, out_ref):
    core = place_ref[1]
    for y in range(mine_ref.shape[0] // size):
        rows = slice(y * size, (y + 1) * size)
        out_ref[aligned(CORES * y + core, size)] = mine_ref[rows]
        out_ref[aligned(CORES * y + 1 - core, size)] = other_ref[rows]


def weight_grad_kernel(other, share, place_ref, received_ref, delta_ref, out_ref):
    core = 1 - place_ref[1] if other else place_ref[1]
    delta = delta_ref[...]
    batch = min(4, out_ref.shape[0] // share)
    for first in range(0, out_ref.shape[0] // share, batch):
        columns = [
            received_ref[:, aligned(CORES * y + core, share)] for y in range(first, first + batch)
        ]
        grad = transposed_times(jnp.concatenate(columns, axis=1), delta)
        out_ref[first * share : (first + batch) * share] = grad.astype(jnp.bfloat16)


def place_back(place_ref, k, count):
    return lax.rem(place_ref[0] + k + count, count)


def add_kernel(place_ref, mine_ref, other_ref, sum_ref, up_ref, down_ref):
    total = mine_ref[...].astype(jnp.float32) + other_ref[...].astype(jnp.float32)
    sum_ref[...] = total.astype(jnp.bfloat16)
    size = up_ref.shape[0]
    ys = sum_ref.shape[0] // size
    up_ref[...] = sum_ref[aligned(place_back(place_ref, ys // 2, ys), size)]
    down_ref[...] = sum_ref[aligned(place_back(place_ref, 1 - ys // 2, ys), size)]


def pass_kernel(ks, place_ref, sum_ref, *refs):
    size = refs[0].shape[0]
    ys = sum_ref.shape[0] // size
    for k, arrived_ref, out_ref in zip(ks, refs[: len(ks)], refs[len(ks) :]):
        own = sum_ref[aligned(place_back(place_ref, k, ys), size)]
        total = arrived_ref[...].astype(jnp.float32) + own.astype(jnp.float32)
        out_ref[...] = total.astype(jnp.bfloat16)


def total_kernel(groups, place_ref, sum_ref, up_ref, down_ref, gate_grad_ref, up_grad_ref):
    hidden = gate_grad_ref.shape[1]
    total = sum_ref[aligned(place_ref[0], up_ref.shape[0])].astype(jnp.float32)
    total += up_ref[...].astype(jnp.float32)
    total += down_ref[...].astype(jnp.float32)
    total *= 1.0 / groups
    gate_grad_ref[...] = total[:, :hidden]
    up_grad_ref[...] = total[:, hidden:]


def whole():
    return pl.BlockSpec(memory_space=pltpu.VMEM)


def anywhere():
    return pl.BlockSpec(memory_space=pl.ANY)


def hbm(array):
    return pltpu.with_memory_space_constraint(array, pltpu.HBM)


def call(kernel, out_shape, flops, moved, vmem=VMEM, **more):
    return pl.pallas_call(
        kernel,
        out_shape=out_shape,
        compiler_params=pltpu.CompilerParams(vmem_limit_bytes=vmem),
        cost_estimate=pl.CostEstimate(flops=flops, bytes_accessed=moved, transcendentals=0),
        **more,
    )


def held_and_sems(shape, count):
    return [pltpu.VMEM(shape, jnp.bfloat16), pltpu.SemaphoreType.DMA((count,))]


def on_device(tokens, routes, cotangent, gate_weight, up_weight):
    peers = lax.axis_size("expert")
    groups = lax.axis_size("dp")
    ys = groups // CORES
    count, width = tokens.shape
    top = routes.shape[1]
    hidden = cotangent.shape[2]
    share = width // groups
    half = width // 2
    bf16 = jnp.bfloat16
    rows = peers * BLOCK
    routes = routes.T
    mine = lax.axis_index("dp")
    place = jnp.stack((mine // CORES, mine % CORES)).astype(jnp.int32)
    scalars = pl.BlockSpec(memory_space=pltpu.SMEM)

    def shape(*dims, kind=bf16):
        return jax.ShapeDtypeStruct(dims, kind)

    def exchange(block, size):
        out = lax.all_to_all(
            block.reshape(peers, size, -1), "expert", split_axis=0, concat_axis=0, tiled=True
        )
        return out.reshape(peers * size, -1)

    def along_y(block, k):
        pairs = [
            (y * CORES + c, (y + k) % ys * CORES + c) for y in range(ys) for c in range(CORES)
        ]
        return lax.ppermute(block, "dp", pairs)

    def other_core(block):
        return lax.ppermute(block, "dp", [(d, d ^ 1) for d in range(groups)])

    packed = call(
        lambda *refs: pack_kernel(peers, *refs),
        pltpu.HBM((rows, width), bf16),
        2 * 10**9,
        5 * 10**6,
        BIG,
        in_specs=[whole(), anywhere(), anywhere()],
        out_specs=anywhere(),
        scratch_shapes=[
            *held_and_sems((rows, width), PER_ROW + 1),
            pltpu.VMEM((count, width), bf16),
            *held_and_sems((count * top, hidden), 2),
        ],
    )(routes, hbm(tokens), hbm(cotangent.reshape(count * top, hidden)))
    received = exchange(packed, BLOCK)
    stacked = call(
        stack_kernel,
        shape(share, 2 * hidden),
        2 * 10**9,
        10**6,
        in_specs=[whole()] * 2,
        out_specs=whole(),
    )(gate_weight[0], up_weight[0])
    blocks = [stacked] + [along_y(stacked, k) for k in range(1, ys)]
    of_core = call(
        collect_kernel,
        shape(ys * share, 2 * hidden),
        10**6,
        3 * 10**6,
        in_specs=[scalars] + [whole()] * ys,
        out_specs=whole(),
    )(place, *blocks)
    weight = call(
        lambda *refs: assemble_kernel(share, *refs),
        shape(width, 2 * hidden),
        10**6,
        6 * 10**6,
        in_specs=[scalars] + [whole()] * 2,
        out_specs=whole(),
    )(place, of_core, other_core(of_core))
    delta, back = call(
        middle_kernel,
        (pltpu.HBM((rows, 2 * hidden), bf16), pltpu.HBM((peers * BACK, half), bf16)),
        5 * 10**9,
        10**7,
        MIDDLE,
        in_specs=[whole(), anywhere()],
        out_specs=(anywhere(), anywhere()),
        scratch_shapes=[
            *held_and_sems((width, 2 * hidden), FETCHES),
            *held_and_sems((rows, 2 * hidden), STEPS),
            *held_and_sems((peers * BACK, half), STEPS),
            pltpu.VMEM((rows, 2 * hidden), jnp.float32),
        ],
    )(received, hbm(weight))
    returned = exchange(back, BACK)
    grads = [
        call(
            lambda *refs, other=other: weight_grad_kernel(other, share, *refs),
            shape(ys * share, 2 * hidden),
            2 * 10**9,
            5 * 10**6,
            in_specs=[scalars] + [whole()] * 2,
            out_specs=whole(),
        )(place, received, delta)
        for other in (True, False)
    ]
    block = shape(share, 2 * hidden)
    summed, up, down = call(
        add_kernel,
        (shape(ys * share, 2 * hidden), block, block),
        10**6,
        5 * 10**6,
        in_specs=[scalars] + [whole()] * 2,
        out_specs=(whole(),) * 3,
    )(place, grads[1], other_core(grads[0]))
    for hop in range(1, ys // 2 + 1):
        up = along_y(up, 1)
        travelling, ks = (up,), (ys // 2 - hop,)
        if hop < ys // 2:
            down = along_y(down, -1)
            travelling, ks = (up, down), (ks[0], hop + 1 - ys // 2)
        if hop == ys // 2:
            break
        if hop == ys // 2 - 1:
            travelling, ks = travelling[:1], ks[:1]
        out = call(
            lambda *refs, ks=ks: pass_kernel(ks, *refs),
            (block,) * len(ks),
            10**5,
            10**6,
            in_specs=[scalars] + [whole()] * (1 + len(ks)),
            out_specs=(whole(),) * len(ks),
        )(place, summed, *travelling)
        up, down = out[0], out[1] if len(ks) == 2 else down
    weight_shape = shape(share, hidden, kind=jnp.float32)
    gate_grad, up_grad = call(
        lambda *refs: total_kernel(groups, *refs),
        (weight_shape, weight_shape),
        10**6,
        2 * 10**6,
        in_specs=[scalars] + [whole()] * 3,
        out_specs=(whole(), whole()),
    )(place, summed, up, down)
    token_grad = call(
        lambda *refs: combine_kernel(peers, *refs),
        shape(count, width),
        10**9,
        4 * 10**6,
        in_specs=[whole()] * 2,
        out_specs=whole(),
    )(routes, returned)
    return (token_grad, gate_grad[None], up_grad[None])


def solution(mesh):
    placed = (
        P(("dp", "expert"), None),
        P(("dp", "expert"), None),
        P(("dp", "expert"), None, None),
        P("expert", "dp", None),
        P("expert", "dp", None),
    )
    return jax.shard_map(
        on_device,
        mesh=mesh,
        in_specs=placed,
        out_specs=(P(("dp", "expert"), None), P("expert", "dp", None), P("expert", "dp", None)),
        check_vma=False,
    )
```

```python
import jax
import jax.numpy as jnp
from jax import lax
from jax.experimental import pallas as pl
from jax.experimental.pallas import tpu as pltpu
from jax.sharding import PartitionSpec as P

CAP = 20
BLOCK = 24
TAIL = 4
PER_ROW = 5
BACK = 40
STEPS = 2
PIECES = 4
CORES = 2
FETCHES = 4
RETURNED = 5
VMEM = 32 * 2**20
BIG = 60 * 2**20
MIDDLE = 32 * 2**20


def iota(shape, axis):
    return lax.broadcasted_iota(jnp.int32, shape, axis)


def one_if(condition):
    return jnp.where(condition, 1.0, 0.0).astype(jnp.bfloat16)


def dot(left, right):
    return jnp.dot(left, right, preferred_element_type=jnp.float32)


def times_transposed(left, right):
    return lax.dot_general(
        left, right, (((1,), (1,)), ((), ())), preferred_element_type=jnp.float32
    )


def transposed_times(left, right):
    return lax.dot_general(
        left, right, (((0,), (0,)), ((), ())), preferred_element_type=jnp.float32
    )


def ranks(routes, experts):
    top, count = routes.shape
    expert = iota((experts, count), 0)
    routed = jnp.zeros((experts, count), jnp.float32)
    for k in range(top):
        routed += jnp.where(routes[k : k + 1, :] == expert, 1.0, 0.0)
    earlier = one_if(iota((count, count), 0) < iota((count, count), 1))
    rank = dot(routed.astype(jnp.bfloat16), earlier)
    return rank, jnp.where(routed > 0.5, rank, -1.0)


def pack_kernel(experts, routes_ref, tokens_hbm, cot_hbm, out_ref, held, sems, tokens_ref, cot_ref, in_sems):
    fetches = (
        pltpu.make_async_copy(tokens_hbm, tokens_ref, in_sems.at[0]),
        pltpu.make_async_copy(cot_hbm, cot_ref, in_sems.at[1]),
    )
    for fetch in fetches:
        fetch.start()
    routes = routes_ref[...]
    top, count = routes.shape
    width = tokens_ref.shape[1]
    hidden = cot_ref.shape[1]
    rank, place = ranks(routes, experts)
    row = iota((BLOCK, count), 0).astype(jnp.float32)
    pick = jnp.concatenate(
        [
            jnp.where(jnp.broadcast_to(place[e : e + 1], row.shape) == row, 1.0, 0.0)
            for e in range(experts)
        ],
        axis=0,
    ).astype(jnp.bfloat16)
    slots = count * top
    spread = one_if(lax.shift_right_logical(iota((count, slots), 1), 3) == iota((count, slots), 0))
    both = jnp.concatenate((routes.astype(jnp.float32), rank), axis=0).astype(jnp.bfloat16)
    wide = dot(both, spread)
    own = iota((top, slots), 0) == (iota((top, slots), 1) & (top - 1))
    named = jnp.sum(jnp.where(own, wide[:top], 0.0), axis=0, keepdims=True)
    slot_place = jnp.where(
        named == iota((experts, slots), 0).astype(jnp.float32), wide[top:], -8.0
    )
    upper = iota((8, slots), 0) < TAIL
    behind = (iota((8, slots), 0) & (TAIL - 1)).astype(jnp.float32)
    offset = jnp.concatenate(
        [
            jnp.where(
                upper,
                jnp.broadcast_to(slot_place[e : e + 1], upper.shape),
                jnp.broadcast_to(slot_place[e + 1 : e + 2], upper.shape),
            )
            - behind
            for e in range(0, experts, 2)
        ],
        axis=0,
    )
    fetches[0].wait()
    copies = []
    for i in (PER_ROW, *range(PER_ROW)):
        low, high = i * hidden, min((i + 1) * hidden, width)
        rows = dot(pick, tokens_ref[:, low:high])
        if i == 0:
            fetches[1].wait()
        if i < PER_ROW:
            tail = dot(one_if(offset == float(TAIL * i)), cot_ref[...])
            tail = tail.reshape(experts // 2, 8, hidden)
            tail = jnp.stack((pltpu.roll(tail, TAIL, 1), tail), axis=1).reshape(experts, 8, hidden)
            rows = rows.reshape(experts, BLOCK, hidden)
            last = rows[:, BLOCK - 8 :]
            last = jnp.where(iota(last.shape, 1) < TAIL, last, tail)
            rows = jnp.concatenate((rows[:, : BLOCK - 8], last), axis=1)
            rows = rows.reshape(experts * BLOCK, hidden)
        held[:, low:high] = rows.astype(jnp.bfloat16)
        at = pl.ds(low, high - low)
        copy = pltpu.make_async_copy(held.at[:, at], out_ref.at[:, at], sems.at[i])
        copy.start()
        copies.append(copy)
    for copy in copies:
        copy.wait()


def stack_kernel(gate_ref, up_ref, stacked_ref):
    stacked_ref[...] = jnp.concatenate((gate_ref[...], up_ref[...]), axis=1)


def combine_kernel(experts, routes_ref, returned_hbm, out_ref, returned_ref, sems):
    half = returned_ref.shape[1]
    count = sems.shape[0]
    size = returned_ref.shape[0] // count
    fetches = []
    for k in range(count):
        at = pl.ds(k * size, size)
        fetch = pltpu.make_async_copy(returned_hbm.at[at], returned_ref.at[at], sems.at[k])
        fetch.start()
        fetches.append(fetch)
    _, place = ranks(routes_ref[...], experts)
    lane = iota((experts, experts * BACK), 1)
    first = iota((experts, experts * BACK), 0) * BACK
    mine = (lane >= first) & (lane < first + BACK)
    at = dot(place.T.astype(jnp.bfloat16), one_if(mine))
    within = jnp.sum(jnp.where(mine, lane - first, 0), axis=0, keepdims=True).astype(jnp.float32)
    low = jnp.where(within < CAP, within, -2.0)
    high = jnp.where(within < BLOCK, within - TAIL, within - BLOCK)
    high = jnp.where(within < CAP, -2.0, high)
    both = jnp.concatenate((one_if(at == low), one_if(at == high)), axis=0)
    total = 0.0
    for k, fetch in enumerate(fetches):
        fetch.wait()
        part = slice(k * size, (k + 1) * size)
        total += dot(both[:, part], returned_ref[part])
    count = out_ref.shape[0]
    out_ref[:, :half] = total[:count].astype(jnp.bfloat16)
    out_ref[:, half:] = total[count:].astype(jnp.bfloat16)


def make_deltas(received, pre):
    rows, hidden = received.shape[0], pre.shape[1] // 2
    blocks = rows // BLOCK
    tail = received[:, : PER_ROW * hidden].astype(jnp.float32)
    tail = tail.reshape(blocks, BLOCK, PER_ROW * hidden)[:, BLOCK - 8 :]
    first = iota((blocks, 8, hidden), 1) < TAIL

    def cot(i):
        return tail[:, :, i * hidden : (i + 1) * hidden]

    grad_out = jnp.concatenate(
        (
            jnp.where(first, pltpu.roll(cot(0), TAIL, 1), cot(1)),
            jnp.where(first, pltpu.roll(cot(2), TAIL, 1), cot(3)),
            jnp.where(first, pltpu.roll(cot(4), TAIL, 1), 0.0),
        ),
        axis=1,
    ).reshape(rows, hidden)
    gate_pre, up_pre = pre[:, :hidden], pre[:, hidden:]
    sigmoid_gate = jax.nn.sigmoid(gate_pre)
    gate_delta = grad_out * up_pre * sigmoid_gate * (1.0 + gate_pre * (1.0 - sigmoid_gate))
    up_delta = grad_out * gate_pre * sigmoid_gate
    return jnp.concatenate((gate_delta, up_delta), axis=1)


def middle_kernel(
    received_ref, weight_hbm, delta_hbm, back_hbm, weight_ref, in_sems, delta_ref, delta_sems, held, sems, pre_ref, twice_ref
):
    width = received_ref.shape[1]
    half = width // 2
    full = BLOCK - 8
    depth = width // FETCHES
    fetches, copies = [], []
    for k in range(FETCHES):
        at = pl.ds(k * depth, depth)
        fetch = pltpu.make_async_copy(weight_hbm.at[at], weight_ref.at[at], in_sems.at[k])
        fetch.start()
        fetches.append(fetch)
    rows = received_ref.shape[0] // STEPS
    for k, fetch in enumerate(fetches):
        fetch.wait()
        at = slice(k * depth, (k + 1) * depth)
        for step in range(STEPS):
            part = slice(step * rows, (step + 1) * rows)
            pre = dot(received_ref[part, at], weight_ref[at])
            if k:
                pre += pre_ref[part]
            if k < FETCHES - 1:
                pre_ref[part] = pre
                continue
            delta = make_deltas(received_ref[part], pre)
            delta_ref[part] = delta.astype(jnp.bfloat16)
            copy = pltpu.make_async_copy(
                delta_ref.at[pl.ds(step * rows, rows)], delta_hbm.at[pl.ds(step * rows, rows)], delta_sems.at[step]
            )
            copy.start()
            copies.append(copy)
            delta = delta.reshape(rows // BLOCK, BLOCK, delta.shape[1])
            last = delta[:, full:]
            last = jnp.where(iota(last.shape, 1) < TAIL, last, pltpu.roll(last, TAIL, 1))
            delta = jnp.concatenate((delta[:, :full], last), axis=1)
            twice_ref[part] = delta.reshape(rows, delta.shape[2]).astype(jnp.bfloat16)
    twice = twice_ref[...]
    blocks = twice.shape[0] // BLOCK
    piece = half // PIECES
    for index in range(PIECES):
        start = index * piece
        low = times_transposed(twice, weight_ref[start : start + piece])
        high = times_transposed(twice, weight_ref[half + start : half + start + piece])
        low = low.reshape(blocks, BLOCK, piece)
        high = high.reshape(blocks, BLOCK, piece)
        shared = jnp.where(iota((blocks, 8, piece), 1) < TAIL, low[:, full:], high[:, full:])
        back = jnp.concatenate((low[:, :full], shared, high[:, :full]), axis=1)
        held[:, start : start + piece] = back.reshape(blocks * BACK, piece).astype(jnp.bfloat16)
        at = pl.ds(start, piece)
        copy = pltpu.make_async_copy(held.at[:, at], back_hbm.at[:, at], sems.at[index])
        copy.start()
        copies.append(copy)
    for copy in copies:
        copy.wait()


def aligned(index, size):
    return pl.ds(pl.multiple_of(index * size, size), size)


def collect_kernel(place_ref, *refs):
    *blocks, out_ref = refs
    size = blocks[0].shape[0]
    for k, block in enumerate(blocks):
        at = lax.rem(place_ref[0] + len(blocks) - k, len(blocks))
        out_ref[aligned(at, size)] = block[...]


def assemble_kernel(size, place_ref, mine_ref, other_ref, out_ref):
    core = place_ref[1]
    for y in range(mine_ref.shape[0] // size):
        rows = slice(y * size, (y + 1) * size)
        out_ref[aligned(CORES * y + core, size)] = mine_ref[rows]
        out_ref[aligned(CORES * y + 1 - core, size)] = other_ref[rows]


def weight_grad_kernel(other, share, place_ref, received_ref, delta_ref, out_ref):
    core = 1 - place_ref[1] if other else place_ref[1]
    delta = delta_ref[...]
    batch = min(4, out_ref.shape[0] // share)
    for first in range(0, out_ref.shape[0] // share, batch):
        columns = [
            received_ref[:, aligned(CORES * y + core, share)] for y in range(first, first + batch)
        ]
        grad = transposed_times(jnp.concatenate(columns, axis=1), delta)
        out_ref[first * share : (first + batch) * share] = grad.astype(jnp.bfloat16)


def place_back(place_ref, k, count):
    return lax.rem(place_ref[0] + k + count, count)


def add_kernel(place_ref, mine_ref, other_ref, sum_ref, up_ref, down_ref):
    total = mine_ref[...].astype(jnp.float32) + other_ref[...].astype(jnp.float32)
    sum_ref[...] = total.astype(jnp.bfloat16)
    size = up_ref.shape[0]
    ys = sum_ref.shape[0] // size
    up_ref[...] = sum_ref[aligned(place_back(place_ref, ys // 2, ys), size)]
    down_ref[...] = sum_ref[aligned(place_back(place_ref, 1 - ys // 2, ys), size)]


def pass_kernel(ks, place_ref, sum_ref, *refs):
    size = refs[0].shape[0]
    ys = sum_ref.shape[0] // size
    for k, arrived_ref, out_ref in zip(ks, refs[: len(ks)], refs[len(ks) :]):
        own = sum_ref[aligned(place_back(place_ref, k, ys), size)]
        total = arrived_ref[...].astype(jnp.float32) + own.astype(jnp.float32)
        out_ref[...] = total.astype(jnp.bfloat16)


def total_kernel(groups, place_ref, sum_ref, up_ref, down_ref, gate_grad_ref, up_grad_ref):
    hidden = gate_grad_ref.shape[1]
    total = sum_ref[aligned(place_ref[0], up_ref.shape[0])].astype(jnp.float32)
    total += up_ref[...].astype(jnp.float32)
    total += down_ref[...].astype(jnp.float32)
    total *= 1.0 / groups
    gate_grad_ref[...] = total[:, :hidden]
    up_grad_ref[...] = total[:, hidden:]


def whole():
    return pl.BlockSpec(memory_space=pltpu.VMEM)


def anywhere():
    return pl.BlockSpec(memory_space=pl.ANY)


def hbm(array):
    return pltpu.with_memory_space_constraint(array, pltpu.HBM)


def call(kernel, out_shape, flops, moved, vmem=VMEM, **more):
    return pl.pallas_call(
        kernel,
        out_shape=out_shape,
        compiler_params=pltpu.CompilerParams(vmem_limit_bytes=vmem),
        cost_estimate=pl.CostEstimate(flops=flops, bytes_accessed=moved, transcendentals=0),
        **more,
    )


def held_and_sems(shape, count):
    return [pltpu.VMEM(shape, jnp.bfloat16), pltpu.SemaphoreType.DMA((count,))]


def on_device(tokens, routes, cotangent, gate_weight, up_weight):
    peers = lax.axis_size("expert")
    groups = lax.axis_size("dp")
    ys = groups // CORES
    count, width = tokens.shape
    top = routes.shape[1]
    hidden = cotangent.shape[2]
    share = width // groups
    half = width // 2
    bf16 = jnp.bfloat16
    rows = peers * BLOCK
    routes = routes.T
    mine = lax.axis_index("dp")
    place = jnp.stack((mine // CORES, mine % CORES)).astype(jnp.int32)
    scalars = pl.BlockSpec(memory_space=pltpu.SMEM)

    def shape(*dims, kind=bf16):
        return jax.ShapeDtypeStruct(dims, kind)

    def exchange(block, size):
        out = lax.all_to_all(
            block.reshape(peers, size, -1), "expert", split_axis=0, concat_axis=0, tiled=True
        )
        return out.reshape(peers * size, -1)

    def along_y(block, k):
        pairs = [
            (y * CORES + c, (y + k) % ys * CORES + c) for y in range(ys) for c in range(CORES)
        ]
        return lax.ppermute(block, "dp", pairs)

    def other_core(block):
        return lax.ppermute(block, "dp", [(d, d ^ 1) for d in range(groups)])

    packed = call(
        lambda *refs: pack_kernel(peers, *refs),
        pltpu.HBM((rows, width), bf16),
        2 * 10**9,
        5 * 10**6,
        BIG,
        in_specs=[whole(), anywhere(), anywhere()],
        out_specs=anywhere(),
        scratch_shapes=[
            *held_and_sems((rows, width), PER_ROW + 1),
            pltpu.VMEM((count, width), bf16),
            *held_and_sems((count * top, hidden), 2),
        ],
    )(routes, hbm(tokens), hbm(cotangent.reshape(count * top, hidden)))
    received = exchange(packed, BLOCK)
    stacked = call(
        stack_kernel,
        shape(share, 2 * hidden),
        2 * 10**9,
        10**6,
        in_specs=[whole()] * 2,
        out_specs=whole(),
    )(gate_weight[0], up_weight[0])
    blocks = [stacked] + [along_y(stacked, k) for k in range(1, ys)]
    of_core = call(
        collect_kernel,
        shape(ys * share, 2 * hidden),
        10**6,
        3 * 10**6,
        in_specs=[scalars] + [whole()] * ys,
        out_specs=whole(),
    )(place, *blocks)
    weight = call(
        lambda *refs: assemble_kernel(share, *refs),
        shape(width, 2 * hidden),
        10**6,
        6 * 10**6,
        in_specs=[scalars] + [whole()] * 2,
        out_specs=whole(),
    )(place, of_core, other_core(of_core))
    delta, back = call(
        middle_kernel,
        (pltpu.HBM((rows, 2 * hidden), bf16), pltpu.HBM((peers * BACK, half), bf16)),
        5 * 10**9,
        10**7,
        MIDDLE,
        in_specs=[whole(), anywhere()],
        out_specs=(anywhere(), anywhere()),
        scratch_shapes=[
            *held_and_sems((width, 2 * hidden), FETCHES),
            *held_and_sems((rows, 2 * hidden), STEPS),
            *held_and_sems((peers * BACK, half), PIECES),
            pltpu.VMEM((rows, 2 * hidden), jnp.float32),
            pltpu.VMEM((rows, 2 * hidden), bf16),
        ],
    )(received, hbm(weight))
    returned = exchange(back, BACK)
    grads = [
        call(
            lambda *refs, other=other: weight_grad_kernel(other, share, *refs),
            shape(ys * share, 2 * hidden),
            2 * 10**9,
            5 * 10**6,
            in_specs=[scalars] + [whole()] * 2,
            out_specs=whole(),
        )(place, received, delta)
        for other in (True, False)
    ]
    block = shape(share, 2 * hidden)
    summed, up, down = call(
        add_kernel,
        (shape(ys * share, 2 * hidden), block, block),
        10**6,
        5 * 10**6,
        in_specs=[scalars] + [whole()] * 2,
        out_specs=(whole(),) * 3,
    )(place, grads[1], other_core(grads[0]))
    for hop in range(1, ys // 2 + 1):
        up = along_y(up, 1)
        travelling, ks = (up,), (ys // 2 - hop,)
        if hop < ys // 2:
            down = along_y(down, -1)
            travelling, ks = (up, down), (ks[0], hop + 1 - ys // 2)
        if hop == ys // 2:
            break
        if hop == ys // 2 - 1:
            travelling, ks = travelling[:1], ks[:1]
        out = call(
            lambda *refs, ks=ks: pass_kernel(ks, *refs),
            (block,) * len(ks),
            10**5,
            10**6,
            in_specs=[scalars] + [whole()] * (1 + len(ks)),
            out_specs=(whole(),) * len(ks),
        )(place, summed, *travelling)
        up, down = out[0], out[1] if len(ks) == 2 else down
    weight_shape = shape(share, hidden, kind=jnp.float32)
    gate_grad, up_grad = call(
        lambda *refs: total_kernel(groups, *refs),
        (weight_shape, weight_shape),
        10**6,
        2 * 10**6,
        in_specs=[scalars] + [whole()] * 3,
        out_specs=(whole(), whole()),
    )(place, summed, up, down)
    token_grad = call(
        lambda *refs: combine_kernel(peers, *refs),
        shape(count, width),
        10**9,
        4 * 10**6,
        in_specs=[whole(), anywhere()],
        out_specs=whole(),
        scratch_shapes=held_and_sems((peers * BACK, half), RETURNED),
    )(routes, hbm(returned))
    return (token_grad, gate_grad[None], up_grad[None])


def solution(mesh):
    placed = (
        P(("dp", "expert"), None),
        P(("dp", "expert"), None),
        P(("dp", "expert"), None, None),
        P("expert", "dp", None),
        P("expert", "dp", None),
    )
    return jax.shard_map(
        on_device,
        mesh=mesh,
        in_specs=placed,
        out_specs=(P(("dp", "expert"), None), P("expert", "dp", None), P("expert", "dp", None)),
        check_vma=False,
    )
```

```python
import jax
import jax.numpy as jnp
from jax import lax
from jax.experimental import pallas as pl
from jax.experimental.pallas import tpu as pltpu
from jax.sharding import PartitionSpec as P

CAP = 20
BLOCK = 24
TAIL = 4
PER_ROW = 5
BACK = 40
STEPS = 2
PIECES = 4
CORES = 2
FETCHES = 4
VMEM = 32 * 2**20
BIG = 60 * 2**20
MIDDLE = 32 * 2**20


def iota(shape, axis):
    return lax.broadcasted_iota(jnp.int32, shape, axis)


def one_if(condition):
    return jnp.where(condition, 1.0, 0.0).astype(jnp.bfloat16)


def dot(left, right):
    return jnp.dot(left, right, preferred_element_type=jnp.float32)


def times_transposed(left, right):
    return lax.dot_general(
        left, right, (((1,), (1,)), ((), ())), preferred_element_type=jnp.float32
    )


def transposed_times(left, right):
    return lax.dot_general(
        left, right, (((0,), (0,)), ((), ())), preferred_element_type=jnp.float32
    )


def ranks(routes, experts):
    top, count = routes.shape
    expert = iota((experts, count), 0)
    routed = jnp.zeros((experts, count), jnp.float32)
    for k in range(top):
        routed += jnp.where(routes[k : k + 1, :] == expert, 1.0, 0.0)
    earlier = one_if(iota((count, count), 0) < iota((count, count), 1))
    rank = dot(routed.astype(jnp.bfloat16), earlier)
    return rank, jnp.where(routed > 0.5, rank, -1.0)


def pack_kernel(experts, routes_hbm, tokens_hbm, cot_hbm, out_ref, held, sems, tokens_ref, cot_ref, in_sems, routes_ref):
    fetches = (
        pltpu.make_async_copy(routes_hbm, routes_ref, in_sems.at[2]),
        pltpu.make_async_copy(tokens_hbm, tokens_ref, in_sems.at[0]),
        pltpu.make_async_copy(cot_hbm, cot_ref, in_sems.at[1]),
    )
    for fetch in fetches:
        fetch.start()
    fetches[0].wait()
    routes = routes_ref[...]
    top, count = routes.shape
    width = tokens_ref.shape[1]
    hidden = cot_ref.shape[1]
    rank, place = ranks(routes, experts)
    row = iota((BLOCK, count), 0).astype(jnp.float32)
    pick = jnp.concatenate(
        [
            jnp.where(jnp.broadcast_to(place[e : e + 1], row.shape) == row, 1.0, 0.0)
            for e in range(experts)
        ],
        axis=0,
    ).astype(jnp.bfloat16)
    slots = count * top
    spread = one_if(lax.shift_right_logical(iota((count, slots), 1), 3) == iota((count, slots), 0))
    both = jnp.concatenate((routes.astype(jnp.float32), rank), axis=0).astype(jnp.bfloat16)
    wide = dot(both, spread)
    own = iota((top, slots), 0) == (iota((top, slots), 1) & (top - 1))
    named = jnp.sum(jnp.where(own, wide[:top], 0.0), axis=0, keepdims=True)
    slot_place = jnp.where(
        named == iota((experts, slots), 0).astype(jnp.float32), wide[top:], -8.0
    )
    upper = iota((8, slots), 0) < TAIL
    behind = (iota((8, slots), 0) & (TAIL - 1)).astype(jnp.float32)
    offset = jnp.concatenate(
        [
            jnp.where(
                upper,
                jnp.broadcast_to(slot_place[e : e + 1], upper.shape),
                jnp.broadcast_to(slot_place[e + 1 : e + 2], upper.shape),
            )
            - behind
            for e in range(0, experts, 2)
        ],
        axis=0,
    )
    fetches[1].wait()
    copies = []
    for i in (PER_ROW, *range(PER_ROW)):
        low, high = i * hidden, min((i + 1) * hidden, width)
        rows = dot(pick, tokens_ref[:, low:high])
        if i == 0:
            fetches[2].wait()
        if i < PER_ROW:
            tail = dot(one_if(offset == float(TAIL * i)), cot_ref[...])
            tail = tail.reshape(experts // 2, 8, hidden)
            tail = jnp.stack((pltpu.roll(tail, TAIL, 1), tail), axis=1).reshape(experts, 8, hidden)
            rows = rows.reshape(experts, BLOCK, hidden)
            last = rows[:, BLOCK - 8 :]
            last = jnp.where(iota(last.shape, 1) < TAIL, last, tail)
            rows = jnp.concatenate((rows[:, : BLOCK - 8], last), axis=1)
            rows = rows.reshape(experts * BLOCK, hidden)
        held[:, low:high] = rows.astype(jnp.bfloat16)
        at = pl.ds(low, high - low)
        copy = pltpu.make_async_copy(held.at[:, at], out_ref.at[:, at], sems.at[i])
        copy.start()
        copies.append(copy)
    for copy in copies:
        copy.wait()


def stack_kernel(gate_ref, up_ref, stacked_ref):
    stacked_ref[...] = jnp.concatenate((gate_ref[...], up_ref[...]), axis=1)


def combine_kernel(experts, routes_ref, returned_ref, out_ref):
    half = returned_ref.shape[1]
    _, place = ranks(routes_ref[...], experts)
    lane = iota((experts, experts * BACK), 1)
    first = iota((experts, experts * BACK), 0) * BACK
    mine = (lane >= first) & (lane < first + BACK)
    at = dot(place.T.astype(jnp.bfloat16), one_if(mine))
    within = jnp.sum(jnp.where(mine, lane - first, 0), axis=0, keepdims=True).astype(jnp.float32)
    low = jnp.where(within < CAP, within, -2.0)
    high = jnp.where(within < BLOCK, within - TAIL, within - BLOCK)
    high = jnp.where(within < CAP, -2.0, high)
    both = jnp.concatenate((one_if(at == low), one_if(at == high)), axis=0)
    total = dot(both, returned_ref[...])
    count = out_ref.shape[0]
    out_ref[:, :half] = total[:count].astype(jnp.bfloat16)
    out_ref[:, half:] = total[count:].astype(jnp.bfloat16)


def make_deltas(received, pre):
    rows, hidden = received.shape[0], pre.shape[1] // 2
    blocks = rows // BLOCK
    tail = received[:, : PER_ROW * hidden].astype(jnp.float32)
    tail = tail.reshape(blocks, BLOCK, PER_ROW * hidden)[:, BLOCK - 8 :]
    first = iota((blocks, 8, hidden), 1) < TAIL

    def cot(i):
        return tail[:, :, i * hidden : (i + 1) * hidden]

    grad_out = jnp.concatenate(
        (
            jnp.where(first, pltpu.roll(cot(0), TAIL, 1), cot(1)),
            jnp.where(first, pltpu.roll(cot(2), TAIL, 1), cot(3)),
            jnp.where(first, pltpu.roll(cot(4), TAIL, 1), 0.0),
        ),
        axis=1,
    ).reshape(rows, hidden)
    gate_pre, up_pre = pre[:, :hidden], pre[:, hidden:]
    sigmoid_gate = jax.nn.sigmoid(gate_pre)
    gate_delta = grad_out * up_pre * sigmoid_gate * (1.0 + gate_pre * (1.0 - sigmoid_gate))
    up_delta = grad_out * gate_pre * sigmoid_gate
    return jnp.concatenate((gate_delta, up_delta), axis=1)


def middle_kernel(
    received_ref, weight_hbm, delta_hbm, back_hbm, kept_hbm, weight_ref, in_sems, delta_ref, delta_sems, held, sems, pre_ref, twice_ref, kept_sem
):
    width = received_ref.shape[1]
    half = width // 2
    full = BLOCK - 8
    depth = width // FETCHES
    fetches, copies = [], []
    for k in range(FETCHES):
        at = pl.ds(k * depth, depth)
        fetch = pltpu.make_async_copy(weight_hbm.at[at], weight_ref.at[at], in_sems.at[k])
        fetch.start()
        fetches.append(fetch)
    rows = received_ref.shape[0] // STEPS
    for k, fetch in enumerate(fetches):
        fetch.wait()
        if k == FETCHES - 1:
            keep = pltpu.make_async_copy(received_ref, kept_hbm, kept_sem.at[0])
            keep.start()
            copies.append(keep)
        at = slice(k * depth, (k + 1) * depth)
        for step in range(STEPS):
            part = slice(step * rows, (step + 1) * rows)
            pre = dot(received_ref[part, at], weight_ref[at])
            if k:
                pre += pre_ref[part]
            if k < FETCHES - 1:
                pre_ref[part] = pre
                continue
            delta = make_deltas(received_ref[part], pre)
            delta_ref[part] = delta.astype(jnp.bfloat16)
            copy = pltpu.make_async_copy(
                delta_ref.at[pl.ds(step * rows, rows)], delta_hbm.at[pl.ds(step * rows, rows)], delta_sems.at[step]
            )
            copy.start()
            copies.append(copy)
            delta = delta.reshape(rows // BLOCK, BLOCK, delta.shape[1])
            last = delta[:, full:]
            last = jnp.where(iota(last.shape, 1) < TAIL, last, pltpu.roll(last, TAIL, 1))
            delta = jnp.concatenate((delta[:, :full], last), axis=1)
            twice_ref[part] = delta.reshape(rows, delta.shape[2]).astype(jnp.bfloat16)
    twice = twice_ref[...]
    blocks = twice.shape[0] // BLOCK
    piece = half // PIECES
    for index in range(PIECES):
        start = index * piece
        low = times_transposed(twice, weight_ref[start : start + piece])
        high = times_transposed(twice, weight_ref[half + start : half + start + piece])
        low = low.reshape(blocks, BLOCK, piece)
        high = high.reshape(blocks, BLOCK, piece)
        shared = jnp.where(iota((blocks, 8, piece), 1) < TAIL, low[:, full:], high[:, full:])
        back = jnp.concatenate((low[:, :full], shared, high[:, :full]), axis=1)
        held[:, start : start + piece] = back.reshape(blocks * BACK, piece).astype(jnp.bfloat16)
        at = pl.ds(start, piece)
        copy = pltpu.make_async_copy(held.at[:, at], back_hbm.at[:, at], sems.at[index])
        copy.start()
        copies.append(copy)
    for copy in copies:
        copy.wait()


def aligned(index, size):
    return pl.ds(pl.multiple_of(index * size, size), size)


def collect_kernel(place_ref, *refs):
    *blocks, out_ref = refs
    size = blocks[0].shape[0]
    for k, block in enumerate(blocks):
        at = lax.rem(place_ref[0] + len(blocks) - k, len(blocks))
        out_ref[aligned(at, size)] = block[...]


def assemble_kernel(size, place_ref, mine_ref, other_ref, out_ref):
    core = place_ref[1]
    for y in range(mine_ref.shape[0] // size):
        rows = slice(y * size, (y + 1) * size)
        out_ref[aligned(CORES * y + core, size)] = mine_ref[rows]
        out_ref[aligned(CORES * y + 1 - core, size)] = other_ref[rows]


def weight_grad_kernel(other, share, place_ref, received_ref, delta_ref, out_ref):
    core = 1 - place_ref[1] if other else place_ref[1]
    delta = delta_ref[...]
    batch = min(4, out_ref.shape[0] // share)
    for first in range(0, out_ref.shape[0] // share, batch):
        columns = [
            received_ref[:, aligned(CORES * y + core, share)] for y in range(first, first + batch)
        ]
        grad = transposed_times(jnp.concatenate(columns, axis=1), delta)
        out_ref[first * share : (first + batch) * share] = grad.astype(jnp.bfloat16)


def place_back(place_ref, k, count):
    return lax.rem(place_ref[0] + k + count, count)


def add_kernel(place_ref, mine_ref, other_ref, sum_ref, up_ref, down_ref):
    total = mine_ref[...].astype(jnp.float32) + other_ref[...].astype(jnp.float32)
    sum_ref[...] = total.astype(jnp.bfloat16)
    size = up_ref.shape[0]
    ys = sum_ref.shape[0] // size
    up_ref[...] = sum_ref[aligned(place_back(place_ref, ys // 2, ys), size)]
    down_ref[...] = sum_ref[aligned(place_back(place_ref, 1 - ys // 2, ys), size)]


def pass_kernel(ks, place_ref, sum_ref, *refs):
    size = refs[0].shape[0]
    ys = sum_ref.shape[0] // size
    for k, arrived_ref, out_ref in zip(ks, refs[: len(ks)], refs[len(ks) :]):
        own = sum_ref[aligned(place_back(place_ref, k, ys), size)]
        total = arrived_ref[...].astype(jnp.float32) + own.astype(jnp.float32)
        out_ref[...] = total.astype(jnp.bfloat16)


def total_kernel(groups, place_ref, sum_ref, up_ref, down_ref, gate_grad_ref, up_grad_ref):
    hidden = gate_grad_ref.shape[1]
    total = sum_ref[aligned(place_ref[0], up_ref.shape[0])].astype(jnp.float32)
    total += up_ref[...].astype(jnp.float32)
    total += down_ref[...].astype(jnp.float32)
    total *= 1.0 / groups
    gate_grad_ref[...] = total[:, :hidden]
    up_grad_ref[...] = total[:, hidden:]


def whole():
    return pl.BlockSpec(memory_space=pltpu.VMEM)


def anywhere():
    return pl.BlockSpec(memory_space=pl.ANY)


def hbm(array):
    return pltpu.with_memory_space_constraint(array, pltpu.HBM)


def call(kernel, out_shape, flops, moved, vmem=VMEM, **more):
    return pl.pallas_call(
        kernel,
        out_shape=out_shape,
        compiler_params=pltpu.CompilerParams(vmem_limit_bytes=vmem),
        cost_estimate=pl.CostEstimate(flops=flops, bytes_accessed=moved, transcendentals=0),
        **more,
    )


def held_and_sems(shape, count):
    return [pltpu.VMEM(shape, jnp.bfloat16), pltpu.SemaphoreType.DMA((count,))]


def on_device(tokens, routes, cotangent, gate_weight, up_weight):
    peers = lax.axis_size("expert")
    groups = lax.axis_size("dp")
    ys = groups // CORES
    count, width = tokens.shape
    top = routes.shape[1]
    hidden = cotangent.shape[2]
    share = width // groups
    half = width // 2
    bf16 = jnp.bfloat16
    rows = peers * BLOCK
    routes = routes.T
    mine = lax.axis_index("dp")
    place = jnp.stack((mine // CORES, mine % CORES)).astype(jnp.int32)
    scalars = pl.BlockSpec(memory_space=pltpu.SMEM)

    def shape(*dims, kind=bf16):
        return jax.ShapeDtypeStruct(dims, kind)

    def exchange(block, size):
        out = lax.all_to_all(
            block.reshape(peers, size, -1), "expert", split_axis=0, concat_axis=0, tiled=True
        )
        return out.reshape(peers * size, -1)

    def along_y(block, k):
        pairs = [
            (y * CORES + c, (y + k) % ys * CORES + c) for y in range(ys) for c in range(CORES)
        ]
        return lax.ppermute(block, "dp", pairs)

    def other_core(block):
        return lax.ppermute(block, "dp", [(d, d ^ 1) for d in range(groups)])

    packed = call(
        lambda *refs: pack_kernel(peers, *refs),
        pltpu.HBM((rows, width), bf16),
        2 * 10**9,
        5 * 10**6,
        BIG,
        in_specs=[anywhere()] * 3,
        out_specs=anywhere(),
        scratch_shapes=[
            *held_and_sems((rows, width), PER_ROW + 1),
            pltpu.VMEM((count, width), bf16),
            *held_and_sems((count * top, hidden), 3),
            pltpu.VMEM((top, count), jnp.int32),
        ],
    )(hbm(routes), hbm(tokens), hbm(cotangent.reshape(count * top, hidden)))
    received = exchange(packed, BLOCK)
    stacked = call(
        stack_kernel,
        shape(share, 2 * hidden),
        2 * 10**9,
        10**6,
        in_specs=[whole()] * 2,
        out_specs=whole(),
    )(gate_weight[0], up_weight[0])
    blocks = [stacked] + [along_y(stacked, k) for k in range(1, ys)]
    of_core = call(
        collect_kernel,
        shape(ys * share, 2 * hidden),
        10**6,
        3 * 10**6,
        in_specs=[scalars] + [whole()] * ys,
        out_specs=whole(),
    )(place, *blocks)
    weight = call(
        lambda *refs: assemble_kernel(share, *refs),
        shape(width, 2 * hidden),
        10**6,
        6 * 10**6,
        in_specs=[scalars] + [whole()] * 2,
        out_specs=whole(),
    )(place, of_core, other_core(of_core))
    delta, back, kept = call(
        middle_kernel,
        (
            pltpu.HBM((rows, 2 * hidden), bf16),
            pltpu.HBM((peers * BACK, half), bf16),
            pltpu.HBM((rows, width), bf16),
        ),
        5 * 10**9,
        10**7,
        MIDDLE,
        in_specs=[whole(), anywhere()],
        out_specs=(anywhere(),) * 3,
        scratch_shapes=[
            *held_and_sems((width, 2 * hidden), FETCHES),
            *held_and_sems((rows, 2 * hidden), STEPS),
            *held_and_sems((peers * BACK, half), PIECES),
            pltpu.VMEM((rows, 2 * hidden), jnp.float32),
            pltpu.VMEM((rows, 2 * hidden), bf16),
            pltpu.SemaphoreType.DMA((1,)),
        ],
    )(received, hbm(weight))
    returned = exchange(back, BACK)
    grads = [
        call(
            lambda *refs, other=other: weight_grad_kernel(other, share, *refs),
            shape(ys * share, 2 * hidden),
            2 * 10**9,
            5 * 10**6,
            in_specs=[scalars] + [whole()] * 2,
            out_specs=whole(),
        )(place, kept, delta)
        for other in (True, False)
    ]
    block = shape(share, 2 * hidden)
    summed, up, down = call(
        add_kernel,
        (shape(ys * share, 2 * hidden), block, block),
        10**6,
        5 * 10**6,
        in_specs=[scalars] + [whole()] * 2,
        out_specs=(whole(),) * 3,
    )(place, grads[1], other_core(grads[0]))
    for hop in range(1, ys // 2 + 1):
        up = along_y(up, 1)
        travelling, ks = (up,), (ys // 2 - hop,)
        if hop < ys // 2:
            down = along_y(down, -1)
            travelling, ks = (up, down), (ks[0], hop + 1 - ys // 2)
        if hop == ys // 2:
            break
        if hop == ys // 2 - 1:
            travelling, ks = travelling[:1], ks[:1]
        out = call(
            lambda *refs, ks=ks: pass_kernel(ks, *refs),
            (block,) * len(ks),
            10**5,
            10**6,
            in_specs=[scalars] + [whole()] * (1 + len(ks)),
            out_specs=(whole(),) * len(ks),
        )(place, summed, *travelling)
        up, down = out[0], out[1] if len(ks) == 2 else down
    weight_shape = shape(share, hidden, kind=jnp.float32)
    gate_grad, up_grad = call(
        lambda *refs: total_kernel(groups, *refs),
        (weight_shape, weight_shape),
        10**6,
        2 * 10**6,
        in_specs=[scalars] + [whole()] * 3,
        out_specs=(whole(), whole()),
    )(place, summed, up, down)
    token_grad = call(
        lambda *refs: combine_kernel(peers, *refs),
        shape(count, width),
        10**9,
        4 * 10**6,
        in_specs=[whole()] * 2,
        out_specs=whole(),
    )(routes, returned)
    return (token_grad, gate_grad[None], up_grad[None])


def solution(mesh):
    placed = (
        P(("dp", "expert"), None),
        P(("dp", "expert"), None),
        P(("dp", "expert"), None, None),
        P("expert", "dp", None),
        P("expert", "dp", None),
    )
    return jax.shard_map(
        on_device,
        mesh=mesh,
        in_specs=placed,
        out_specs=(P(("dp", "expert"), None), P("expert", "dp", None), P("expert", "dp", None)),
        check_vma=False,
    )
```

```python
import jax
import jax.numpy as jnp
from jax import lax
from jax.experimental import pallas as pl
from jax.experimental.pallas import tpu as pltpu
from jax.sharding import PartitionSpec as P

CAP = 20
BLOCK = 24
TAIL = 4
PER_ROW = 5
BACK = 40
STEPS = 2
PIECES = 4
CORES = 2
FETCHES = (1, 2, 2, 3)
VMEM = 32 * 2**20
BIG = 60 * 2**20
MIDDLE = 32 * 2**20


def iota(shape, axis):
    return lax.broadcasted_iota(jnp.int32, shape, axis)


def one_if(condition):
    return jnp.where(condition, 1.0, 0.0).astype(jnp.bfloat16)


def dot(left, right):
    return jnp.dot(left, right, preferred_element_type=jnp.float32)


def times_transposed(left, right):
    return lax.dot_general(
        left, right, (((1,), (1,)), ((), ())), preferred_element_type=jnp.float32
    )


def transposed_times(left, right):
    return lax.dot_general(
        left, right, (((0,), (0,)), ((), ())), preferred_element_type=jnp.float32
    )


def ranks(routes, experts):
    top, count = routes.shape
    expert = iota((experts, count), 0)
    routed = jnp.zeros((experts, count), jnp.float32)
    for k in range(top):
        routed += jnp.where(routes[k : k + 1, :] == expert, 1.0, 0.0)
    earlier = one_if(iota((count, count), 0) < iota((count, count), 1))
    rank = dot(routed.astype(jnp.bfloat16), earlier)
    return rank, jnp.where(routed > 0.5, rank, -1.0)


def pack_kernel(experts, routes_hbm, tokens_hbm, cot_hbm, out_ref, held, sems, tokens_ref, cot_ref, in_sems, routes_ref):
    fetches = (
        pltpu.make_async_copy(routes_hbm, routes_ref, in_sems.at[2]),
        pltpu.make_async_copy(tokens_hbm, tokens_ref, in_sems.at[0]),
        pltpu.make_async_copy(cot_hbm, cot_ref, in_sems.at[1]),
    )
    for fetch in fetches:
        fetch.start()
    fetches[0].wait()
    routes = routes_ref[...]
    top, count = routes.shape
    width = tokens_ref.shape[1]
    hidden = cot_ref.shape[1]
    rank, place = ranks(routes, experts)
    row = iota((BLOCK, count), 0).astype(jnp.float32)
    pick = jnp.concatenate(
        [
            jnp.where(jnp.broadcast_to(place[e : e + 1], row.shape) == row, 1.0, 0.0)
            for e in range(experts)
        ],
        axis=0,
    ).astype(jnp.bfloat16)
    slots = count * top
    spread = one_if(lax.shift_right_logical(iota((count, slots), 1), 3) == iota((count, slots), 0))
    both = jnp.concatenate((routes.astype(jnp.float32), rank), axis=0).astype(jnp.bfloat16)
    wide = dot(both, spread)
    own = iota((top, slots), 0) == (iota((top, slots), 1) & (top - 1))
    named = jnp.sum(jnp.where(own, wide[:top], 0.0), axis=0, keepdims=True)
    slot_place = jnp.where(
        named == iota((experts, slots), 0).astype(jnp.float32), wide[top:], -8.0
    )
    upper = iota((8, slots), 0) < TAIL
    behind = (iota((8, slots), 0) & (TAIL - 1)).astype(jnp.float32)
    offset = jnp.concatenate(
        [
            jnp.where(
                upper,
                jnp.broadcast_to(slot_place[e : e + 1], upper.shape),
                jnp.broadcast_to(slot_place[e + 1 : e + 2], upper.shape),
            )
            - behind
            for e in range(0, experts, 2)
        ],
        axis=0,
    )
    fetches[1].wait()
    copies = []
    for i in (PER_ROW, *range(PER_ROW)):
        low, high = i * hidden, min((i + 1) * hidden, width)
        rows = dot(pick, tokens_ref[:, low:high])
        if i == 0:
            fetches[2].wait()
        if i < PER_ROW:
            tail = dot(one_if(offset == float(TAIL * i)), cot_ref[...])
            tail = tail.reshape(experts // 2, 8, hidden)
            tail = jnp.stack((pltpu.roll(tail, TAIL, 1), tail), axis=1).reshape(experts, 8, hidden)
            rows = rows.reshape(experts, BLOCK, hidden)
            last = rows[:, BLOCK - 8 :]
            last = jnp.where(iota(last.shape, 1) < TAIL, last, tail)
            rows = jnp.concatenate((rows[:, : BLOCK - 8], last), axis=1)
            rows = rows.reshape(experts * BLOCK, hidden)
        held[:, low:high] = rows.astype(jnp.bfloat16)
        at = pl.ds(low, high - low)
        copy = pltpu.make_async_copy(held.at[:, at], out_ref.at[:, at], sems.at[i])
        copy.start()
        copies.append(copy)
    for copy in copies:
        copy.wait()


def stack_kernel(gate_ref, up_ref, stacked_ref):
    stacked_ref[...] = jnp.concatenate((gate_ref[...], up_ref[...]), axis=1)


def matrix_kernel(experts, routes_ref, after_ref, out_ref):
    _, place = ranks(routes_ref[...], experts)
    lane = iota((experts, experts * BACK), 1)
    first = iota((experts, experts * BACK), 0) * BACK
    mine = (lane >= first) & (lane < first + BACK)
    at = dot(place.T.astype(jnp.bfloat16), one_if(mine))
    within = jnp.sum(jnp.where(mine, lane - first, 0), axis=0, keepdims=True).astype(jnp.float32)
    low = jnp.where(within < CAP, within, -2.0)
    high = jnp.where(within < BLOCK, within - TAIL, within - BLOCK)
    high = jnp.where(within < CAP, -2.0, high)
    out_ref[...] = jnp.concatenate((one_if(at == low), one_if(at == high)), axis=0)


def combine_kernel(matrix_ref, returned_ref, out_ref):
    half = returned_ref.shape[1]
    total = dot(matrix_ref[...], returned_ref[...])
    count = out_ref.shape[0]
    out_ref[:, :half] = total[:count].astype(jnp.bfloat16)
    out_ref[:, half:] = total[count:].astype(jnp.bfloat16)


def make_deltas(received, pre):
    rows, hidden = received.shape[0], pre.shape[1] // 2
    blocks = rows // BLOCK
    tail = received[:, : PER_ROW * hidden].astype(jnp.float32)
    tail = tail.reshape(blocks, BLOCK, PER_ROW * hidden)[:, BLOCK - 8 :]
    first = iota((blocks, 8, hidden), 1) < TAIL

    def cot(i):
        return tail[:, :, i * hidden : (i + 1) * hidden]

    grad_out = jnp.concatenate(
        (
            jnp.where(first, pltpu.roll(cot(0), TAIL, 1), cot(1)),
            jnp.where(first, pltpu.roll(cot(2), TAIL, 1), cot(3)),
            jnp.where(first, pltpu.roll(cot(4), TAIL, 1), 0.0),
        ),
        axis=1,
    ).reshape(rows, hidden)
    gate_pre, up_pre = pre[:, :hidden], pre[:, hidden:]
    sigmoid_gate = jax.nn.sigmoid(gate_pre)
    gate_delta = grad_out * up_pre * sigmoid_gate * (1.0 + gate_pre * (1.0 - sigmoid_gate))
    up_delta = grad_out * gate_pre * sigmoid_gate
    return jnp.concatenate((gate_delta, up_delta), axis=1)


def middle_kernel(
    received_ref, weight_hbm, delta_hbm, back_hbm, kept_hbm, weight_ref, in_sems, delta_ref, delta_sems, held, sems, pre_ref, twice_ref, kept_sem
):
    width = received_ref.shape[1]
    half = width // 2
    full = BLOCK - 8
    unit = width // sum(FETCHES)
    starts = [unit * sum(FETCHES[:k]) for k in range(len(FETCHES) + 1)]
    fetches, copies = [], []
    for k in range(len(FETCHES)):
        at = pl.ds(starts[k], starts[k + 1] - starts[k])
        fetch = pltpu.make_async_copy(weight_hbm.at[at], weight_ref.at[at], in_sems.at[k])
        fetch.start()
        fetches.append(fetch)
    rows = received_ref.shape[0] // STEPS
    for k, fetch in enumerate(fetches):
        fetch.wait()
        if k == len(FETCHES) - 1:
            keep = pltpu.make_async_copy(received_ref, kept_hbm, kept_sem.at[0])
            keep.start()
            copies.append(keep)
        at = slice(starts[k], starts[k + 1])
        for step in range(STEPS):
            part = slice(step * rows, (step + 1) * rows)
            pre = dot(received_ref[part, at], weight_ref[at])
            if k:
                pre += pre_ref[part]
            if k < len(FETCHES) - 1:
                pre_ref[part] = pre
                continue
            delta = make_deltas(received_ref[part], pre)
            delta_ref[part] = delta.astype(jnp.bfloat16)
            copy = pltpu.make_async_copy(
                delta_ref.at[pl.ds(step * rows, rows)], delta_hbm.at[pl.ds(step * rows, rows)], delta_sems.at[step]
            )
            copy.start()
            copies.append(copy)
            delta = delta.reshape(rows // BLOCK, BLOCK, delta.shape[1])
            last = delta[:, full:]
            last = jnp.where(iota(last.shape, 1) < TAIL, last, pltpu.roll(last, TAIL, 1))
            delta = jnp.concatenate((delta[:, :full], last), axis=1)
            twice_ref[part] = delta.reshape(rows, delta.shape[2]).astype(jnp.bfloat16)
    twice = twice_ref[...]
    blocks = twice.shape[0] // BLOCK
    piece = half // PIECES
    for index in range(PIECES):
        start = index * piece
        low = times_transposed(twice, weight_ref[start : start + piece])
        high = times_transposed(twice, weight_ref[half + start : half + start + piece])
        low = low.reshape(blocks, BLOCK, piece)
        high = high.reshape(blocks, BLOCK, piece)
        shared = jnp.where(iota((blocks, 8, piece), 1) < TAIL, low[:, full:], high[:, full:])
        back = jnp.concatenate((low[:, :full], shared, high[:, :full]), axis=1)
        held[:, start : start + piece] = back.reshape(blocks * BACK, piece).astype(jnp.bfloat16)
        at = pl.ds(start, piece)
        copy = pltpu.make_async_copy(held.at[:, at], back_hbm.at[:, at], sems.at[index])
        copy.start()
        copies.append(copy)
    for copy in copies:
        copy.wait()


def aligned(index, size):
    return pl.ds(pl.multiple_of(index * size, size), size)


def collect_kernel(place_ref, *refs):
    *blocks, out_ref = refs
    size = blocks[0].shape[0]
    for k, block in enumerate(blocks):
        at = lax.rem(place_ref[0] + len(blocks) - k, len(blocks))
        out_ref[aligned(at, size)] = block[...]


def assemble_kernel(size, place_ref, mine_ref, other_ref, out_ref):
    core = place_ref[1]
    for y in range(mine_ref.shape[0] // size):
        rows = slice(y * size, (y + 1) * size)
        out_ref[aligned(CORES * y + core, size)] = mine_ref[rows]
        out_ref[aligned(CORES * y + 1 - core, size)] = other_ref[rows]


def weight_grad_kernel(other, share, place_ref, received_ref, delta_ref, out_ref):
    core = 1 - place_ref[1] if other else place_ref[1]
    delta = delta_ref[...]
    batch = min(4, out_ref.shape[0] // share)
    for first in range(0, out_ref.shape[0] // share, batch):
        columns = [
            received_ref[:, aligned(CORES * y + core, share)] for y in range(first, first + batch)
        ]
        grad = transposed_times(jnp.concatenate(columns, axis=1), delta)
        out_ref[first * share : (first + batch) * share] = grad.astype(jnp.bfloat16)


def place_back(place_ref, k, count):
    return lax.rem(place_ref[0] + k + count, count)


def add_kernel(place_ref, mine_ref, other_ref, sum_ref, up_ref, down_ref):
    total = mine_ref[...].astype(jnp.float32) + other_ref[...].astype(jnp.float32)
    sum_ref[...] = total.astype(jnp.bfloat16)
    size = up_ref.shape[0]
    ys = sum_ref.shape[0] // size
    up_ref[...] = sum_ref[aligned(place_back(place_ref, ys // 2, ys), size)]
    down_ref[...] = sum_ref[aligned(place_back(place_ref, 1 - ys // 2, ys), size)]


def pass_kernel(ks, place_ref, sum_ref, *refs):
    size = refs[0].shape[0]
    ys = sum_ref.shape[0] // size
    for k, arrived_ref, out_ref in zip(ks, refs[: len(ks)], refs[len(ks) :]):
        own = sum_ref[aligned(place_back(place_ref, k, ys), size)]
        total = arrived_ref[...].astype(jnp.float32) + own.astype(jnp.float32)
        out_ref[...] = total.astype(jnp.bfloat16)


def total_kernel(groups, place_ref, sum_ref, up_ref, down_ref, gate_grad_ref, up_grad_ref):
    hidden = gate_grad_ref.shape[1]
    total = sum_ref[aligned(place_ref[0], up_ref.shape[0])].astype(jnp.float32)
    total += up_ref[...].astype(jnp.float32)
    total += down_ref[...].astype(jnp.float32)
    total *= 1.0 / groups
    gate_grad_ref[...] = total[:, :hidden]
    up_grad_ref[...] = total[:, hidden:]


def whole():
    return pl.BlockSpec(memory_space=pltpu.VMEM)


def anywhere():
    return pl.BlockSpec(memory_space=pl.ANY)


def hbm(array):
    return pltpu.with_memory_space_constraint(array, pltpu.HBM)


def call(kernel, out_shape, flops, moved, vmem=VMEM, **more):
    return pl.pallas_call(
        kernel,
        out_shape=out_shape,
        compiler_params=pltpu.CompilerParams(vmem_limit_bytes=vmem),
        cost_estimate=pl.CostEstimate(flops=flops, bytes_accessed=moved, transcendentals=0),
        **more,
    )


def held_and_sems(shape, count):
    return [pltpu.VMEM(shape, jnp.bfloat16), pltpu.SemaphoreType.DMA((count,))]


def on_device(tokens, routes, cotangent, gate_weight, up_weight):
    peers = lax.axis_size("expert")
    groups = lax.axis_size("dp")
    ys = groups // CORES
    count, width = tokens.shape
    top = routes.shape[1]
    hidden = cotangent.shape[2]
    share = width // groups
    half = width // 2
    bf16 = jnp.bfloat16
    rows = peers * BLOCK
    routes = routes.T
    mine = lax.axis_index("dp")
    place = jnp.stack((mine // CORES, mine % CORES)).astype(jnp.int32)
    scalars = pl.BlockSpec(memory_space=pltpu.SMEM)

    def shape(*dims, kind=bf16):
        return jax.ShapeDtypeStruct(dims, kind)

    def exchange(block, size):
        out = lax.all_to_all(
            block.reshape(peers, size, -1), "expert", split_axis=0, concat_axis=0, tiled=True
        )
        return out.reshape(peers * size, -1)

    def along_y(block, k):
        pairs = [
            (y * CORES + c, (y + k) % ys * CORES + c) for y in range(ys) for c in range(CORES)
        ]
        return lax.ppermute(block, "dp", pairs)

    def other_core(block):
        return lax.ppermute(block, "dp", [(d, d ^ 1) for d in range(groups)])

    packed = call(
        lambda *refs: pack_kernel(peers, *refs),
        pltpu.HBM((rows, width), bf16),
        2 * 10**9,
        5 * 10**6,
        BIG,
        in_specs=[anywhere()] * 3,
        out_specs=anywhere(),
        scratch_shapes=[
            *held_and_sems((rows, width), PER_ROW + 1),
            pltpu.VMEM((count, width), bf16),
            *held_and_sems((count * top, hidden), 3),
            pltpu.VMEM((top, count), jnp.int32),
        ],
    )(hbm(routes), hbm(tokens), hbm(cotangent.reshape(count * top, hidden)))
    received = exchange(packed, BLOCK)
    stacked = call(
        stack_kernel,
        shape(share, 2 * hidden),
        2 * 10**9,
        10**6,
        in_specs=[whole()] * 2,
        out_specs=whole(),
    )(gate_weight[0], up_weight[0])
    blocks = [stacked] + [along_y(stacked, k) for k in range(1, ys)]
    of_core = call(
        collect_kernel,
        shape(ys * share, 2 * hidden),
        10**6,
        3 * 10**6,
        in_specs=[scalars] + [whole()] * ys,
        out_specs=whole(),
    )(place, *blocks)
    weight = call(
        lambda *refs: assemble_kernel(share, *refs),
        shape(width, 2 * hidden),
        10**6,
        6 * 10**6,
        in_specs=[scalars] + [whole()] * 2,
        out_specs=whole(),
    )(place, of_core, other_core(of_core))
    delta, back, kept = call(
        middle_kernel,
        (
            pltpu.HBM((rows, 2 * hidden), bf16),
            pltpu.HBM((peers * BACK, half), bf16),
            pltpu.HBM((rows, width), bf16),
        ),
        5 * 10**9,
        10**7,
        MIDDLE,
        in_specs=[whole(), anywhere()],
        out_specs=(anywhere(),) * 3,
        scratch_shapes=[
            *held_and_sems((width, 2 * hidden), len(FETCHES)),
            *held_and_sems((rows, 2 * hidden), STEPS),
            *held_and_sems((peers * BACK, half), PIECES),
            pltpu.VMEM((rows, 2 * hidden), jnp.float32),
            pltpu.VMEM((rows, 2 * hidden), bf16),
            pltpu.SemaphoreType.DMA((1,)),
        ],
    )(received, hbm(weight))
    returned = exchange(back, BACK)
    grads = [
        call(
            lambda *refs, other=other: weight_grad_kernel(other, share, *refs),
            shape(ys * share, 2 * hidden),
            2 * 10**9,
            5 * 10**6,
            in_specs=[scalars] + [whole()] * 2,
            out_specs=whole(),
        )(place, kept, delta)
        for other in (True, False)
    ]
    block = shape(share, 2 * hidden)
    summed, up, down = call(
        add_kernel,
        (shape(ys * share, 2 * hidden), block, block),
        10**6,
        5 * 10**6,
        in_specs=[scalars] + [whole()] * 2,
        out_specs=(whole(),) * 3,
    )(place, grads[1], other_core(grads[0]))
    for hop in range(1, ys // 2 + 1):
        up = along_y(up, 1)
        travelling, ks = (up,), (ys // 2 - hop,)
        if hop < ys // 2:
            down = along_y(down, -1)
            travelling, ks = (up, down), (ks[0], hop + 1 - ys // 2)
        if hop == ys // 2:
            break
        if hop == ys // 2 - 1:
            travelling, ks = travelling[:1], ks[:1]
        out = call(
            lambda *refs, ks=ks: pass_kernel(ks, *refs),
            (block,) * len(ks),
            10**5,
            10**6,
            in_specs=[scalars] + [whole()] * (1 + len(ks)),
            out_specs=(whole(),) * len(ks),
        )(place, summed, *travelling)
        up, down = out[0], out[1] if len(ks) == 2 else down
    weight_shape = shape(share, hidden, kind=jnp.float32)
    gate_grad, up_grad = call(
        lambda *refs: total_kernel(groups, *refs),
        (weight_shape, weight_shape),
        10**6,
        2 * 10**6,
        in_specs=[scalars] + [whole()] * 3,
        out_specs=(whole(), whole()),
    )(place, summed, up, down)
    matrix = call(
        lambda *refs: matrix_kernel(peers, *refs),
        shape(2 * count, peers * BACK),
        2 * 10**9,
        10**6,
        in_specs=[whole(), anywhere()],
        out_specs=whole(),
    )(routes, gate_grad)
    token_grad = call(
        combine_kernel,
        shape(count, width),
        10**9,
        4 * 10**6,
        in_specs=[whole()] * 2,
        out_specs=whole(),
    )(matrix, returned)
    return (token_grad, gate_grad[None], up_grad[None])


def solution(mesh):
    placed = (
        P(("dp", "expert"), None),
        P(("dp", "expert"), None),
        P(("dp", "expert"), None, None),
        P("expert", "dp", None),
        P("expert", "dp", None),
    )
    return jax.shard_map(
        on_device,
        mesh=mesh,
        in_specs=placed,
        out_specs=(P(("dp", "expert"), None), P("expert", "dp", None), P("expert", "dp", None)),
        check_vma=False,
    )
```
